256 devices in a mesh: frames: 32 (over z_hi, x, core), feats: 8 (over y, z_lo).
Axes of the slice: x: 4, y: 4, z: 8 (z_hi: 4, z_lo: 2; z = z_hi * 2 + z_lo), core: 2. Of those that a mesh axis runs over, the one named last changes fastest.
Arguments:
- frames_data: bfloat16 [49152, 4096], P('frames', 'feats')
- lag_index: int32 [49152], P('frames'), may hold values from 1 to 49151, as said below
- projection: bfloat16 [4096, 64], P('feats'), may hold values from -0.09375 to 0.09375
- center_ids: int32 [256], replicated, may hold values from 0 to 49151
- nearest_prev: float32 [49152], P('frames'), may hold values from 0.5 to 2.5
Outputs:
- instant_cov: float32 [4096, 4096], P('frames', 'feats')
- lagged_cov: float32 [4096, 4096], P('frames', 'feats')
- coords: float32 [64, 49152], P(None, 'frames')
- nearest: float32 [49152], P('frames')
The draws below stay inside these ranges and needn't reach their ends.
Inputs may be any that keep to these rules, and one draw needn't show every extreme that they name: lag_index[r] = min(r + lag[r], 49151), where each frame r has its own lag[r] of 1 to 512 (lags differ from frame to frame); it exceeds r for every frame but the last.
All inputs are finite; a program needn't handle non-finite values.
Results may differ from the reference program's by a relative error of at most 0.0003.
Values may be sent and summed in bfloat16 or wider, within the bound.
A program may use at most 128 MiB of HBM per device.

```python
import jax
import jax.numpy as jnp
from jax import lax

F = 4096
K = 64
C = 256
LAG_MAX = 512
ROWS = 49152


def draw_frames_data(key, part):
    key = jax.random.fold_in(key, 11)
    key_mean, key_noise = jax.random.split(key, 2)
    offsets = jax.random.uniform(key_mean, (F,), jnp.float32, -0.25, 0.25)
    noise = jax.random.normal(key_noise, (ROWS, F), jnp.float32)
    return (offsets[None, :] + noise).astype(jnp.bfloat16)


def draw_lag_index(key, part):
    key = jax.random.fold_in(key, 23)
    lags = jax.random.randint(key, (ROWS,), 1, LAG_MAX + 1, dtype=jnp.int32)
    positions = jnp.arange(ROWS, dtype=jnp.int32)
    return jnp.minimum(positions + lags, ROWS - 1).astype(jnp.int32)


def plant(drawn, stream_key, least, largest):
    shape = drawn.shape
    place = [jax.random.randint(jax.random.fold_in(stream_key, axis), (), 0, shape[axis]) for axis in range(len(shape))]
    drawn = drawn.at[tuple(place)].set(least)
    longest = shape.index(max(shape))
    place[longest] = (place[longest] + 1) % shape[longest]
    return drawn.at[tuple(place)].set(largest)


def levels(key, extent, cuts, low, largest):
    level = 1.0
    for axis_at, blocks in cuts:
        steps = jax.random.uniform(jax.random.fold_in(jax.random.fold_in(key, 6), axis_at), (blocks,), jnp.float32, low / len(cuts), largest / len(cuts))
        level = level * jnp.repeat(jnp.exp(steps), extent[axis_at] // blocks).reshape((-1,) + (1,) * (len(extent) - 1 - axis_at))
    return level


def bell_draw(stream_key, shape, scale, bound, cuts=(), kind=jnp.bfloat16):
    result = scale * jax.random.normal(stream_key, shape, jnp.float32)
    if cuts:
        result = result * levels(stream_key, shape, cuts, -0.22, 0.18)
    return jnp.clip(result, -bound, bound).astype(kind)


def setup_inputs(seed: int = 0) -> dict:
    streams_of = jax.random.split(jax.random.key(seed), 6)
    return {
        "frames_data": draw_frames_data(jax.random.fold_in(streams_of[5], 71), 0),
        "lag_index": draw_lag_index(jax.random.fold_in(streams_of[5], 71), 0),
        "projection": bell_draw(streams_of[2], (F, K), F ** -0.5, 0.09375, ((0, 8),)),
        "center_ids": plant(jax.random.randint(streams_of[3], (C,), 0, ROWS), jax.random.fold_in(streams_of[3], 1), 0, ROWS - 1).astype(jnp.int32),
        "nearest_prev": jnp.clip(0.5 + 2.0 * jax.random.uniform(streams_of[4], (ROWS,), jnp.float32) ** levels(streams_of[4], (ROWS,), ((0, 32),), -0.2, 0.2), 0.5, 2.5),
    }


def reference(frames_data, lag_index, projection, center_ids, nearest_prev):
    data = frames_data.astype(jnp.float32)
    lagged = jnp.take(frames_data, lag_index, axis=0).astype(jnp.float32)
    instant_cov = jnp.dot(data.T, data, precision=lax.Precision.HIGHEST) / ROWS
    lagged_cov = jnp.dot(data.T, lagged, precision=lax.Precision.HIGHEST) / ROWS
    coords = jnp.dot(projection.astype(jnp.float32).T, data.T, precision=lax.Precision.HIGHEST)
    centers = jnp.take(coords, center_ids, axis=1)
    square_y = jnp.sum(coords * coords, axis=0)
    square_c = jnp.sum(centers * centers, axis=0)
    cross = jnp.dot(centers.T, coords, precision=lax.Precision.HIGHEST)
    dist = (square_c[:, None] + square_y[None, :] - 2.0 * cross) / K
    nearest = jnp.minimum(nearest_prev, jnp.min(dist, axis=0))
    return instant_cov, lagged_cov, coords, nearest
```

```python
import functools

import jax
import jax.numpy as jnp
from jax import lax
from jax.experimental import pallas as pl
from jax.experimental.pallas import tpu as pltpu
from jax.sharding import PartitionSpec as P

MESH = pl.DeviceIdType.MESH
F32 = jnp.float32
BF16 = jnp.bfloat16
I16 = jnp.int16

ROWS = 1536
FB = 512
LAG = 512
TOTAL = 49152
K = 64
C = 256
NCH = 6
CH = ROWS // NCH
LEVELS = 32767.0

OFFSETS = ((0, 0), (1, 0), (3, 0), (1, 1))
UNITS = ((0, 0), (1, 0), (2, 0), (1, 2), (3, 0), (0, 3), (1, 3), (2, 3))
LAG_SLOT = {0: 0, 2: 1, 3: 2}
NU = len(UNITS)


def dot(a, b, dims, precision=None):
    return lax.dot_general(a, b, ((dims[:1], dims[1:]), ((), ())), precision=precision, preferred_element_type=F32)


def kernel(
    x_ref, idx_ref, proj_ref, ids_ref, prev_ref,
    inst_ref, lag_ref, coords_ref, near_ref,
    xb, lb, u, cx, s1, s1s, r1, r1s, s2, s2s, r2, r2s, zs, zss, zr, zrs, es, ob,
    cpart, crecv, call, cen, cenr,
    ysend, yrecv, fsend, frecv, hsend, hrecv,
    cxsend, cxrecv, s1send, s1recv, s2send, s2recv, zsend, zrecv, esend, erecv,
    psend, precv, gsend, grecv, nsend, nrecv,
):
    p = lax.axis_index("frames")
    q = lax.axis_index("feats")
    zh, x, c = p // 8, (p // 2) % 4, p % 2
    y, zl = q // 2, q % 2

    def at(zh_, x_, c_):
        return zh_ * 8 + x_ * 2 + c_

    xp = (at(zh, (x + 1) % 4, c), q)
    xm = (at(zh, (x + 3) % 4, c), q)
    core = (at(zh, x, 1 - c), q)
    yp = (p, ((y + 1) % 4) * 2 + zl)
    ym = (p, ((y + 3) % 4) * 2 + zl)
    zo = (p, y * 2 + 1 - zl)
    before = ((p + 31) % 32, q)

    def remote(src, dst, ss, rs, dev):
        return pltpu.make_async_remote_copy(
            src_ref=src, dst_ref=dst, send_sem=ss, recv_sem=rs, device_id=dev, device_id_type=MESH
        )

    sent = []

    def send(src, dst, ss, rs, dev):
        r = remote(src, dst, ss, rs, dev)
        r.start()
        sent.append(r)
        return r

    def part(slot, ch):
        return xb.at[slot, :, pl.ds(ch * CH, CH)]

    def halo(slot):
        return send(xb.at[slot, :, pl.ds(0, LAG)], xb.at[slot, :, pl.ds(ROWS, LAG)],
                    hsend.at[slot], hrecv.at[slot], before)

    y1 = []
    y2 = []
    for ch in range(NCH):
        xb[0, :, pl.ds(ch * CH, CH)] = x_ref[pl.ds(ch * CH, CH), :].T
        y1.append(send(part(0, ch), part(1, ch), ysend.at[0, ch], yrecv.at[0, ch], ym))
        y2.append(send(part(0, ch), part(2, ch), ysend.at[1, ch], yrecv.at[1, ch], yp))
        if (ch + 1) * CH == LAG:
            h0 = halo(0)

    cpart[...] = dot(proj_ref[...], xb[0, :, 0:ROWS], (1, 0))
    qsend = []
    for t in range(1, 8):
        to = (q + t) % 8
        qsend.append(send(cpart.at[pl.ds(pl.multiple_of(to * 8, 8), 8), :], crecv.at[t],
                          psend.at[t], precv.at[t], (p, to)))

    first = p * ROWS

    def gather(slot):
        at_slot = LAG_SLOT[slot]

        def body(i, carry):
            base = pl.multiple_of(i * 256, 256)
            here = idx_ref[:, pl.ds(base, 256)] - (first + base)
            pick = (lax.broadcasted_iota(jnp.int32, (768, 256), 0) == here).astype(F32).astype(BF16)
            lb[at_slot, :, pl.ds(base, 256)] = dot(xb[slot, :, pl.ds(base, 768)], pick, (1, 0)).astype(BF16)
            return carry

        lax.fori_loop(0, ROWS // 256, body, 0)

    h0.wait_recv()
    gather(0)

    def encode(value, out, scale_out):
        top = jnp.maximum(jnp.max(jnp.abs(value), axis=0, keepdims=True), 1e-30)
        scale_out[...] = top * (1.0 / LEVELS)
        out[...] = jnp.round(value * (LEVELS / top)).astype(jnp.int32).astype(I16)

    def decode(code, scale):
        return code[...].astype(jnp.int32).astype(F32) * scale[...]

    cxs, s1w, s2w, zw = {}, {}, {}, {}
    mine = pl.multiple_of(c * 256, 256)
    other = pl.multiple_of((1 - c) * 256, 256)

    def stage0(k):
        a, b = UNITS[k]

        def body(i, carry):
            rows = pl.ds(pl.multiple_of(i * 256, 256), 256)
            left = xb[a, rows, 0:ROWS]
            u[k, rows, 0:FB] = dot(left, xb[b, :, 0:ROWS], (1, 1))
            u[k, rows, FB:2 * FB] = dot(left, lb[LAG_SLOT[b]], (1, 1))
            return carry

        lax.fori_loop(0, 2, body, 0)
        cxs[k] = send(u.at[k, pl.ds(other, 256), :], cx.at[k], cxsend.at[k], cxrecv.at[k], core)

    def slice_of(k, xs):
        return pl.ds(pl.multiple_of(c * 256 + xs * 64, 64), 64)

    def stage1(k):
        cxs[k].wait_recv()
        u[k, pl.ds(mine, 256), :] = u[k, pl.ds(mine, 256), :] + cx[k]
        encode(u[k, slice_of(k, (x + 2) % 4), :], s1.at[k], s1s.at[k])
        out = []
        for j, dev in ((0, xp), (1, xm)):
            out.append(send(s1.at[k, pl.ds(j * 32, 32), :], r1.at[k, pl.ds(j * 32, 32), :],
                            s1send.at[k, j, 0], s1recv.at[k, j, 0], dev))
            out.append(send(s1s.at[k], r1s.at[k, j], s1send.at[k, j, 1], s1recv.at[k, j, 1], dev))
        s1w[k] = out

    def stage2(k):
        for r in s1w[k]:
            r.wait_recv()
        out = []
        for j, dev, xs in ((0, xp, (x + 1) % 4), (1, xm, (x + 3) % 4)):
            value = u[k, slice_of(k, xs), :]
            half = decode(r1.at[k, pl.ds(j * 32, 32), :], r1s.at[k, j])
            near, far = (value[0:32] + half, value[32:64]) if j == 0 else (value[0:32], value[32:64] + half)
            encode(jnp.concatenate([near, far], axis=0), s2.at[k, j], s2s.at[k, j])
            out.append(send(s2.at[k, j], r2.at[k, j], s2send.at[k, j, 0], s2recv.at[k, j, 0], dev))
            out.append(send(s2s.at[k, j], r2s.at[k, j], s2send.at[k, j, 1], s2recv.at[k, j, 1], dev))
        s2w[k] = out

    def stage3(k):
        for r in s2w[k]:
            r.wait_recv()
        rows = slice_of(k, x)
        u[k, rows, :] = u[k, rows, :] + decode(r2.at[k, 0], r2s.at[k, 0]) + decode(r2.at[k, 1], r2s.at[k, 1])
        out = []
        for t in (1, 3, 2):
            to = (zh + t) % 4
            encode(u[k, pl.ds(pl.multiple_of(c * 256 + x * 64 + to * 16, 16), 16), :], zs.at[k, t - 1], zss.at[k, t - 1])
            dev = (at(to, x, c), q)
            out.append(send(zs.at[k, t - 1], zr.at[k, t - 1], zsend.at[k, t - 1, 0], zrecv.at[k, t - 1, 0], dev))
            out.append(send(zss.at[k, t - 1], zrs.at[k, t - 1], zsend.at[k, t - 1, 1], zrecv.at[k, t - 1, 1], dev))
        zw[k] = out

    def stage4(k):
        for r in zw[k]:
            r.wait_recv()
        total = u[k, pl.ds(pl.multiple_of(c * 256 + x * 64 + zh * 16, 16), 16), :]
        for t in range(3):
            total = total + decode(zr.at[k, t], zrs.at[k, t])
        es[k] = total / TOTAL
        a, b = UNITS[k]
        rowblock = ((y + OFFSETS[a][0]) % 4) * 2 + (zl + OFFSETS[a][1]) % 2
        colblock = ((y + OFFSETS[b][0]) % 4) * 2 + (zl + OFFSETS[b][1]) % 2
        owner = rowblock * 4 + c * 2 + x // 2
        place = ob.at[pl.ds(pl.multiple_of((x % 2) * 64 + zh * 16, 16), 16), :]
        if b == 0:
            @pl.when(owner == p)
            def _():
                pltpu.make_async_copy(es.at[k], place, erecv).start()

            @pl.when(owner != p)
            def _():
                remote(es.at[k], place, esend.at[k], erecv, (owner, colblock)).start()
        else:
            remote(es.at[k], place, esend.at[k], erecv, (owner, colblock)).start()

    def finish(k):
        a, b = UNITS[k]
        rowblock = ((y + OFFSETS[a][0]) % 4) * 2 + (zl + OFFSETS[a][1]) % 2
        owner = rowblock * 4 + c * 2 + x // 2
        r = remote(es.at[k], ob.at[pl.ds(0, 16), :], esend.at[k], erecv, core)
        if b == 0:
            @pl.when(owner != p)
            def _():
                r.wait_send()
        else:
            r.wait_send()

    stage0(0)
    fw = []

    def forward(ch):
        y1[ch].wait_recv()
        fw.append(send(part(1, ch), part(3, ch), fsend.at[ch], frecv.at[ch], zo))

    forward(0)
    y2[0].wait_recv()
    forward(1)
    y2[1].wait_recv()
    h2 = halo(2)
    stage1(0)
    own8 = pl.ds(pl.multiple_of(q * 8, 8), 8)
    total = cpart[own8, :]
    for r in qsend:
        r.wait_recv()
    for t in range(1, 8):
        total = total + crecv[t]
    call[own8, :] = total
    gs = []
    for t in range(1, 8):
        gs.append(send(call.at[own8, :], call.at[own8, :], gsend.at[t], grecv.at[t], (p, (q + t) % 8)))
    forward(2)
    stage2(0)
    fw[0].wait_recv()
    fw[1].wait_recv()
    h3 = halo(3)
    forward(3)
    stage3(0)
    for t in range(1, 8):
        frm = pl.ds(pl.multiple_of(((q + 8 - t) % 8) * 8, 8), 8)
        remote(call.at[frm, :], call.at[frm, :], gsend.at[t], grecv.at[t], core).wait_recv()
    coords = call[...]
    coords_ref[...] = coords
    pick = (lax.broadcasted_iota(jnp.int32, (C, ROWS), 1) + first == ids_ref[...]).astype(F32)
    cen[0] = dot(coords, pick, (1, 1), lax.Precision.HIGHEST)
    nc = send(cen.at[0], cenr.at[0], nsend.at[0], nrecv.at[0], core)
    forward(4)
    stage4(0)
    nc.wait_recv()
    cen[1] = cen[0] + cenr[0]
    nx = [send(cen.at[1], cenr.at[t], nsend.at[t], nrecv.at[t], (at(zh, (x + t) % 4, c), q)) for t in range(1, 4)]
    forward(5)
    for r in nx:
        r.wait_recv()
    cen[2] = cen[1] + cenr[1] + cenr[2] + cenr[3]
    nz = [send(cen.at[2], cenr.at[3 + t], nsend.at[3 + t], nrecv.at[3 + t], (at((zh + t) % 4, x, c), q)) for t in range(1, 4)]

    for ch in range(2, NCH):
        y2[ch].wait_recv()

    def nearest():
        for r in nz:
            r.wait_recv()
        centers = cen[2] + cenr[4] + cenr[5] + cenr[6]
        ones = jnp.ones((8, K), F32)
        square_y = jnp.sum(coords_ref[...] * coords_ref[...], axis=0, keepdims=True)
        square_c = dot(centers * centers, ones, (0, 1), lax.Precision.HIGHEST)[:, 0:1]
        cross = dot(centers, coords_ref[...], (0, 0), lax.Precision.HIGHEST)
        dist = (square_c + square_y - 2.0 * cross) * (1.0 / K)
        near_ref[...] = jnp.minimum(prev_ref[...], jnp.min(dist, axis=0, keepdims=True))

    def ready(k):
        if k == 3:
            h2.wait_recv()
            gather(2)
        if k == 4:
            for ch in range(2, NCH):
                fw[ch].wait_recv()
        if k == 5:
            h3.wait_recv()
            gather(3)

    for step in range(1, NU + 4):
        if step >= 5:
            stage4(step - 4)
        if 1 <= step - 3 < NU:
            stage3(step - 3)
        if 1 <= step - 2 < NU:
            stage2(step - 2)
        if 1 <= step - 1 < NU:
            stage1(step - 1)
        if step < NU:
            ready(step)
            stage0(step)
        if step == NU:
            nearest()

    pltpu.make_async_copy(ob, ob, erecv).wait()
    inst_ref[...] = ob[:, 0:FB]
    lag_ref[...] = ob[:, FB:2 * FB]
    for r in sent:
        r.wait_send()
    for k in range(NU):
        finish(k)


def per_device(frames_data, lag_index, projection, center_ids, nearest_prev):
    vmem = pl.BlockSpec(memory_space=pltpu.VMEM)
    dma = pltpu.SemaphoreType.DMA
    wide = 2 * FB
    inst, lagged, coords, nearest = pl.pallas_call(
        kernel,
        out_shape=[
            jax.ShapeDtypeStruct((128, FB), F32),
            jax.ShapeDtypeStruct((128, FB), F32),
            jax.ShapeDtypeStruct((K, ROWS), F32),
            jax.ShapeDtypeStruct((1, ROWS), F32),
        ],
        in_specs=[vmem] * 5,
        out_specs=[vmem] * 4,
        scratch_shapes=[
            pltpu.VMEM((4, FB, ROWS + LAG), BF16),
            pltpu.VMEM((3, FB, ROWS), BF16),
            pltpu.VMEM((NU, FB, wide), F32),
            pltpu.VMEM((NU, 256, wide), F32),
            pltpu.VMEM((NU, 64, wide), I16),
            pltpu.VMEM((NU, 1, wide), F32),
            pltpu.VMEM((NU, 64, wide), I16),
            pltpu.VMEM((NU, 2, 1, wide), F32),
            pltpu.VMEM((NU, 2, 64, wide), I16),
            pltpu.VMEM((NU, 2, 1, wide), F32),
            pltpu.VMEM((NU, 2, 64, wide), I16),
            pltpu.VMEM((NU, 2, 1, wide), F32),
            pltpu.VMEM((NU, 3, 16, wide), I16),
            pltpu.VMEM((NU, 3, 1, wide), F32),
            pltpu.VMEM((NU, 3, 16, wide), I16),
            pltpu.VMEM((NU, 3, 1, wide), F32),
            pltpu.VMEM((NU, 16, wide), F32),
            pltpu.VMEM((128, wide), F32),
            pltpu.VMEM((K, ROWS), F32),
            pltpu.VMEM((8, 8, ROWS), F32),
            pltpu.VMEM((K, ROWS), F32),
            pltpu.VMEM((3, K, C), F32),
            pltpu.VMEM((7, K, C), F32),
            dma((2, NCH)), dma((2, NCH)), dma((NCH,)), dma((NCH,)), dma((4,)), dma((4,)),
            dma((NU,)), dma((NU,)), dma((NU, 2, 2)), dma((NU, 2, 2)), dma((NU, 2, 2)), dma((NU, 2, 2)),
            dma((NU, 3, 2)), dma((NU, 3, 2)), dma((NU,)), dma(()),
            dma((8,)), dma((8,)), dma((8,)), dma((8,)), dma((7,)), dma((7,)),
        ],
        compiler_params=pltpu.CompilerParams(has_side_effects=True, vmem_limit_bytes=60 * 2**20),
        name="tica",
    )(
        frames_data,
        lag_index.reshape(1, ROWS),
        projection.T,
        center_ids.reshape(C, 1),
        nearest_prev.reshape(1, ROWS),
    )
    return inst, lagged, coords, nearest.reshape(ROWS)


def solution(mesh):
    placed = (P("frames", "feats"), P("frames"), P("feats", None), P(), P("frames"))
    return jax.shard_map(
        per_device,
        mesh=mesh,
        in_specs=placed,
        out_specs=(P("frames", "feats"), P("frames", "feats"), P(None, "frames"), P("frames")),
        check_vma=False,
    )
```

```python
import functools

import jax
import jax.numpy as jnp
from jax import lax
from jax.experimental import pallas as pl
from jax.experimental.pallas import tpu as pltpu
from jax.sharding import PartitionSpec as P

MESH = pl.DeviceIdType.MESH
F32 = jnp.float32
BF16 = jnp.bfloat16
I16 = jnp.int16

ROWS = 1536
FB = 512
LAG = 512
TOTAL = 49152
K = 64
C = 256
CH = 256
NCH = ROWS // CH
NALL = (ROWS + LAG) // CH
HF = FB // 2
LEVELS = 32767.0

OFFSETS = ((0, 0), (1, 0), (3, 0), (1, 1))
PAIRS = ((0, 0), (1, 0), (2, 0), (3, 0), (2, 1), (0, 3), (1, 3), (2, 3))
UNITS = ((0, 0, 0), (0, 0, 1), (1, 0, 0), (2, 0, 0), (3, 0, 0), (1, 0, 1), (2, 0, 1), (3, 0, 1)) + tuple(
    (a, b, h) for a, b in PAIRS[4:] for h in (0, 1)
)
LAG_SLOT = {0: 0, 1: 1, 3: 2}
NU = len(UNITS)
XS = 32


def dot(a, b, dims, precision=None):
    return lax.dot_general(a, b, ((dims[:1], dims[1:]), ((), ())), precision=precision, preferred_element_type=F32)


def kernel(
    x_ref, idx_ref, proj_ref, ids_ref, prev_ref,
    inst_ref, lag_ref, coords_ref, near_ref,
    xb, lb, u, cx, s1, s1s, r1, r1s, s2, s2s, r2, r2s, zs, zss, zr, zrs, es, ob,
    cpart, crecv, csum, call, cen, cenr, cenall,
    ysend, yrecv, fsend, frecv, hsend, hrecv,
    cxsend, cxrecv, s1send, s1recv, s2send, s2recv, zsend, zrecv, esend, erecv,
    psend, precv, gsend, grecv, nsend, nrecv, msend, mrecv,
):
    p = lax.axis_index("frames")
    q = lax.axis_index("feats")
    zh, x, c = p // 8, (p // 2) % 4, p % 2
    y, zl = q // 2, q % 2

    def at(zh_, x_, c_):
        return zh_ * 8 + x_ * 2 + c_

    xp = (at(zh, (x + 1) % 4, c), q)
    xm = (at(zh, (x + 3) % 4, c), q)
    core = (at(zh, x, 1 - c), q)

    def yto(t):
        return (p, ((y + t) % 4) * 2 + zl)

    yp, ym = yto(1), yto(3)
    zo = (p, y * 2 + 1 - zl)
    before = ((p + 31) % 32, q)

    def remote(src, dst, ss, rs, dev):
        return pltpu.make_async_remote_copy(
            src_ref=src, dst_ref=dst, send_sem=ss, recv_sem=rs, device_id=dev, device_id_type=MESH
        )

    sent = []

    def send(src, dst, ss, rs, dev):
        r = remote(src, dst, ss, rs, dev)
        r.start()
        sent.append((r, None))
        return r

    def send_if(cond, src, dst, ss, rs, dev):
        r = remote(src, dst, ss, rs, dev)

        @pl.when(cond)
        def _():
            r.start()

        sent.append((r, cond))
        return r

    def part(slot, h, j):
        return xb.at[slot, pl.ds(h * HF, HF), pl.ds(j * CH, CH)]

    def from_y(w, h, j):
        slot = (1, 2)[w]
        return remote(part(0, h, j), part(slot, h, j), ysend.at[w, h, j], yrecv.at[w, h, j], (ym, yp)[w])

    def to_y(w, h, j):
        if j < NCH:
            r = from_y(w, h, j)
            r.start()
            sent.append((r, None))
        else:
            r = from_y(w, h, j)

            @pl.when(c == 1)
            def _():
                r.start()

            sent.append((r, c == 1))

    def on_chip(slot, h, j):
        if j < NALL - NCH:
            k = (0, 1)[slot == 3]
            rs = (yrecv.at[0, h, NCH + j], frecv.at[h, NCH + j])[slot == 3]
            send_if(c == 1, part(slot, h, j), part(slot, h, NCH + j), hsend.at[k, h, j], rs, core)

    def forward(h, j):
        from_y(0, h, j).wait_recv()
        if j < NCH:
            send(part(1, h, j), part(3, h, j), fsend.at[h, j], frecv.at[h, j], zo)
            on_chip(1, h, j)
        else:
            send_if(c == 1, part(1, h, j), part(3, h, j), fsend.at[h, j], frecv.at[h, j], zo)

    def from_z(h, j):
        remote(part(1, h, j), part(3, h, j), fsend.at[h, j], frecv.at[h, j], zo).wait_recv()
        on_chip(3, h, j)

    for j in range(NCH):
        xb[0, :, pl.ds(j * CH, CH)] = x_ref[pl.ds(j * CH, CH), :].T
        if j == 1:
            head = send(xb.at[0, :, pl.ds(0, LAG)], xb.at[0, :, pl.ds(ROWS, LAG)], hsend.at[2, 0, 0], hrecv, before)
        if j < 3:
            to_y(0, 0, j)
            to_y(1, 0, j)

    kq = K // 4
    cpart[...] = dot(proj_ref[...], xb[0, :, 0:ROWS], (1, 0))
    crs = []
    for t in (1, 3, 2):
        rows = pl.ds(pl.multiple_of(((y + t) % 4) * kq, kq), kq)
        crs.append(send(cpart.at[rows, :], crecv.at[t], psend.at[t], precv.at[t], yto(t)))
    for j in range(3, NCH):
        to_y(0, 0, j)
        to_y(1, 0, j)
    own_rows = pl.ds(pl.multiple_of(y * kq, kq), kq)
    first = p * ROWS
    small = {}

    def coords1():
        for r in crs:
            r.wait_recv()
        csum[0] = cpart[own_rows, :] + crecv[1] + crecv[2] + crecv[3]
        small["z"] = send(csum.at[0], csum.at[1], psend.at[4], precv.at[4], zo)

    def coords2():
        small["z"].wait_recv()
        total = csum[0] + csum[1]
        call[own_rows, :] = total
        for t in (1, 3, 2):
            send(call.at[own_rows, :], call.at[own_rows, :], gsend.at[t], grecv.at[t], yto(t))
        pick = (lax.broadcasted_iota(jnp.int32, (ROWS, C), 0) + first == ids_ref[...]).astype(F32)
        cen[0] = dot(total, pick, (1, 0), lax.Precision.HIGHEST)
        small["n"] = [send(cen.at[0], cenr.at[0], nsend.at[0], nrecv.at[0], core)]

    def centers1():
        for r in small["n"]:
            r.wait_recv()
        cen[1] = cen[0] + cenr[0]
        small["n"] = [
            send(cen.at[1], cenr.at[t], nsend.at[t], nrecv.at[t], (at(zh, (x + t) % 4, c), q)) for t in (1, 2, 3)
        ]

    def centers2():
        for r in small["n"]:
            r.wait_recv()
        cen[2] = cen[1] + cenr[1] + cenr[2] + cenr[3]
        small["n"] = [
            send(cen.at[2], cenr.at[3 + t], nsend.at[3 + t], nrecv.at[3 + t], (at((zh + t) % 4, x, c), q))
            for t in (1, 2, 3)
        ]

    def centers3():
        for r in small["n"]:
            r.wait_recv()
        cenall[own_rows, :] = cen[2] + cenr[4] + cenr[5] + cenr[6]
        for t in (1, 3, 2):
            send(cenall.at[own_rows, :], cenall.at[own_rows, :], msend.at[t], mrecv.at[t], yto(t))

    def nearest():
        for t in (1, 2, 3):
            frm = pl.ds(pl.multiple_of(((y + 4 - t) % 4) * kq, kq), kq)
            remote(call.at[frm, :], call.at[frm, :], gsend.at[t], grecv.at[t], core).wait_recv()
            remote(cenall.at[frm, :], cenall.at[frm, :], msend.at[t], mrecv.at[t], core).wait_recv()
        coords = call[...]
        coords_ref[...] = coords
        centers = cenall[...]
        ones = jnp.ones((8, K), F32)
        square_y = jnp.sum(coords * coords, axis=0, keepdims=True)
        square_c = dot(centers * centers, ones, (0, 1), lax.Precision.HIGHEST)[:, 0:1]
        cross = dot(centers, coords, (0, 0), lax.Precision.HIGHEST)
        dist = (square_c + square_y - 2.0 * cross) * (1.0 / K)
        near_ref[...] = jnp.minimum(prev_ref[...], jnp.min(dist, axis=0, keepdims=True))

    def gather(slot, start, size):
        at_slot = LAG_SLOT[slot]
        feats = pl.ds(start, size)

        def body(i, carry):
            base = pl.multiple_of(i * 256, 256)
            here = idx_ref[:, pl.ds(base, 256)] - (first + base)
            pick = (lax.broadcasted_iota(jnp.int32, (768, 256), 0) == here).astype(F32).astype(BF16)
            lb[at_slot, feats, pl.ds(base, 256)] = dot(xb[slot, feats, pl.ds(base, 768)], pick, (1, 0)).astype(BF16)
            return carry

        lax.fori_loop(0, ROWS // 256, body, 0)

    def encode(value, out, scale_out):
        top = jnp.maximum(jnp.max(jnp.abs(value), axis=0, keepdims=True), 1e-30)
        scale_out[...] = top * (1.0 / LEVELS)
        out[...] = jnp.round(value * (LEVELS / top)).astype(jnp.int32).astype(I16)

    def decode(code, scale):
        return code[...].astype(jnp.int32).astype(F32) * scale[...]

    cxs, s1w, s2w = {}, {}, {}
    mine = pl.ds(pl.multiple_of(c * 128, 128), 128)
    other = pl.ds(pl.multiple_of((1 - c) * 128, 128), 128)

    def stage0(k):
        a, b, h = UNITS[k]
        left = xb[a, pl.ds(h * HF, HF), 0:ROWS]
        u[k, :, 0:FB] = dot(left, xb[b, :, 0:ROWS], (1, 1))
        u[k, :, FB:2 * FB] = dot(left, lb[LAG_SLOT[b]], (1, 1))
        cxs[k] = send(u.at[k, other, :], cx.at[k], cxsend.at[k], cxrecv.at[k], core)

    def slice_of(xs):
        return pl.ds(pl.multiple_of(c * 128 + xs * XS, XS), XS)

    def stage1(k):
        cxs[k].wait_recv()
        u[k, mine, :] = u[k, mine, :] + cx[k]
        encode(u[k, slice_of((x + 2) % 4), :], s1.at[k], s1s.at[k])
        out = []
        for j, dev in ((0, xp), (1, xm)):
            rows = pl.ds(j * 16, 16)
            out.append(send(s1.at[k, rows, :], r1.at[k, rows, :], s1send.at[k, j, 0], s1recv.at[k, j, 0], dev))
            out.append(send(s1s.at[k], r1s.at[k, j], s1send.at[k, j, 1], s1recv.at[k, j, 1], dev))
        s1w[k] = out

    def stage2(k):
        for r in s1w[k]:
            r.wait_recv()
        out = []
        for j, dev, xs in ((0, xp, (x + 1) % 4), (1, xm, (x + 3) % 4)):
            value = u[k, slice_of(xs), :]
            half = decode(r1.at[k, pl.ds(j * 16, 16), :], r1s.at[k, j])
            near, far = (value[0:16] + half, value[16:32]) if j == 0 else (value[0:16], value[16:32] + half)
            encode(jnp.concatenate([near, far], axis=0), s2.at[k, j], s2s.at[k, j])
            out.append(send(s2.at[k, j], r2.at[k, j], s2send.at[k, j, 0], s2recv.at[k, j, 0], dev))
            out.append(send(s2s.at[k, j], r2s.at[k, j], s2send.at[k, j, 1], s2recv.at[k, j, 1], dev))
        s2w[k] = out

    def z_owner(k):
        return (y + OFFSETS[UNITS[k][0]][0]) % 4

    def z_sends(k):
        target = z_owner(k)
        t = (zh + 4 - target) % 4 - 1
        dev = (at(target, x, c), q)
        return (
            remote(zs.at[k], zr.at[k, t], zsend.at[k, 0], zrecv.at[k, t, 0], dev),
            remote(zss.at[k], zrs.at[k, t], zsend.at[k, 1], zrecv.at[k, t, 1], dev),
        )

    def stage3(k):
        for r in s2w[k]:
            r.wait_recv()
        rows = slice_of(x)
        total = u[k, rows, :] + decode(r2.at[k, 0], r2s.at[k, 0]) + decode(r2.at[k, 1], r2s.at[k, 1])

        @pl.when(zh != z_owner(k))
        def _():
            encode(total, zs.at[k], zss.at[k])
            for r in z_sends(k):
                r.start()

        @pl.when(zh == z_owner(k))
        def _():
            es[k] = total

    def e_send(k):
        a, b, h = UNITS[k]
        rowblock = z_owner(k) * 2 + (zl + OFFSETS[a][1]) % 2
        colblock = ((y + OFFSETS[b][0]) % 4) * 2 + (zl + OFFSETS[b][1]) % 2
        owner = rowblock * 4 + h * 2 + c
        place = ob.at[pl.ds(pl.multiple_of(x * XS, XS), XS), :]
        return owner, b == 0, place, remote(es.at[k], place, esend.at[k], erecv, (owner, colblock))

    def stage4(k):
        @pl.when(zh == z_owner(k))
        def _():
            total = es[k]
            for t in range(3):
                remote(zs.at[k], zr.at[k, t], zsend.at[k, 0], zrecv.at[k, t, 0], core).wait_recv()
                remote(zss.at[k], zrs.at[k, t], zsend.at[k, 1], zrecv.at[k, t, 1], core).wait_recv()
                total = total + decode(zr.at[k, t], zrs.at[k, t])
            es[k] = total / TOTAL
            owner, own_column, place, r = e_send(k)
            if own_column:
                @pl.when(owner == p)
                def _():
                    pltpu.make_async_copy(es.at[k], place, erecv).start()

                @pl.when(owner != p)
                def _():
                    r.start()
            else:
                r.start()

    def finish(k):
        @pl.when(zh != z_owner(k))
        def _():
            for r in z_sends(k):
                r.wait_send()

        owner, own_column, _, r = e_send(k)
        away = zh == z_owner(k)
        if own_column:
            away = away & (owner != p)

        @pl.when(away)
        def _():
            r.wait_send()

    head.wait_recv()
    gather(0, 0, FB)
    for j in range(NCH, NALL):
        to_y(0, 0, j)
    forward(0, 0)
    stage0(0)
    stage0(1)
    forward(0, 1)
    stage1(0)
    stage1(1)
    for j in range(NCH):
        to_y(0, 1, j)
        to_y(1, 1, j)
    for j in range(NCH, NALL):
        to_y(0, 1, j)
    from_z(0, 0)
    coords1()
    forward(0, 2)
    stage2(0)
    stage2(1)
    from_z(0, 1)
    forward(0, 3)
    stage3(0)
    stage3(1)
    coords2()
    forward(0, 4)
    stage4(0)
    stage4(1)
    forward(0, 5)
    centers1()
    for j in range(NCH):
        from_y(1, 0, j).wait_recv()
    stage0(2)
    stage0(3)
    forward(0, 6)
    stage1(2)
    stage1(3)
    forward(0, 7)
    centers2()
    for j in range(2, NCH):
        from_z(0, j)
    stage0(4)
    forward(1, 0)
    stage2(2)
    stage2(3)
    stage1(4)
    for j in range(NCH, NALL):
        from_z(0, j)
    forward(1, 1)
    gather(1, 0, HF)
    forward(1, 2)
    from_z(1, 0)
    stage3(2)
    stage3(3)
    stage2(4)
    from_z(1, 1)
    forward(1, 3)
    gather(3, 0, HF)
    centers3()
    forward(1, 4)
    stage4(2)
    stage4(3)
    stage3(4)
    forward(1, 5)
    stage4(4)
    forward(1, 6)
    forward(1, 7)
    for j in range(NCH):
        from_y(1, 1, j).wait_recv()

    def ready(k):
        if k == 7:
            for j in range(2, NCH):
                from_z(1, j)
        if k == 8:
            gather(1, HF, HF)
        if k == 10:
            for j in range(NCH, NALL):
                from_z(1, j)
            gather(3, HF, HF)

    for step in range(5, NU + 7):
        if step < NU:
            ready(step)
            stage0(step)
        if 5 <= step - 1 < NU:
            stage1(step - 1)
        if 5 <= step - 3 < NU:
            stage2(step - 3)
        if 5 <= step - 5 < NU:
            stage3(step - 5)
        if 5 <= step - 7 < NU:
            stage4(step - 7)
        if step == NU:
            nearest()

    pltpu.make_async_copy(ob, ob, erecv).wait()
    inst_ref[...] = ob[:, 0:FB]
    lag_ref[...] = ob[:, FB:2 * FB]
    for r, cond in sent:
        if cond is None:
            r.wait_send()
        else:
            @pl.when(cond)
            def _(r=r):
                r.wait_send()
    for k in range(NU):
        finish(k)


def per_device(frames_data, lag_index, projection, center_ids, nearest_prev):
    vmem = pl.BlockSpec(memory_space=pltpu.VMEM)
    dma = pltpu.SemaphoreType.DMA
    wide = 2 * FB
    inst, lagged, coords, nearest = pl.pallas_call(
        kernel,
        out_shape=[
            jax.ShapeDtypeStruct((128, FB), F32),
            jax.ShapeDtypeStruct((128, FB), F32),
            jax.ShapeDtypeStruct((K, ROWS), F32),
            jax.ShapeDtypeStruct((1, ROWS), F32),
        ],
        in_specs=[vmem] * 5,
        out_specs=[vmem] * 4,
        scratch_shapes=[
            pltpu.VMEM((4, FB, ROWS + LAG), BF16),
            pltpu.VMEM((3, FB, ROWS), BF16),
            pltpu.VMEM((NU, HF, wide), F32),
            pltpu.VMEM((NU, 128, wide), F32),
            pltpu.VMEM((NU, XS, wide), I16),
            pltpu.VMEM((NU, 1, wide), F32),
            pltpu.VMEM((NU, XS, wide), I16),
            pltpu.VMEM((NU, 2, 1, wide), F32),
            pltpu.VMEM((NU, 2, XS, wide), I16),
            pltpu.VMEM((NU, 2, 1, wide), F32),
            pltpu.VMEM((NU, 2, XS, wide), I16),
            pltpu.VMEM((NU, 2, 1, wide), F32),
            pltpu.VMEM((NU, XS, wide), I16),
            pltpu.VMEM((NU, 1, wide), F32),
            pltpu.VMEM((NU, 3, XS, wide), I16),
            pltpu.VMEM((NU, 3, 1, wide), F32),
            pltpu.VMEM((NU, XS, wide), F32),
            pltpu.VMEM((128, wide), F32),
            pltpu.VMEM((K, ROWS), F32),
            pltpu.VMEM((4, K // 4, ROWS), F32),
            pltpu.VMEM((2, K // 4, ROWS), F32),
            pltpu.VMEM((K, ROWS), F32),
            pltpu.VMEM((3, K // 4, C), F32),
            pltpu.VMEM((7, K // 4, C), F32),
            pltpu.VMEM((K, C), F32),
            dma((2, 2, NALL)), dma((2, 2, NALL)), dma((2, NALL)), dma((2, NALL)), dma((3, 2, 2)), dma(()),
            dma((NU,)), dma((NU,)), dma((NU, 2, 2)), dma((NU, 2, 2)), dma((NU, 2, 2)), dma((NU, 2, 2)),
            dma((NU, 2)), dma((NU, 3, 2)), dma((NU,)), dma(()),
            dma((5,)), dma((5,)), dma((4,)), dma((4,)), dma((7,)), dma((7,)), dma((4,)), dma((4,)),
        ],
        compiler_params=pltpu.CompilerParams(has_side_effects=True, vmem_limit_bytes=60 * 2**20),
        name="tica",
    )(
        frames_data,
        lag_index.reshape(1, ROWS),
        projection.T,
        center_ids.reshape(1, C),
        nearest_prev.reshape(1, ROWS),
    )
    return inst, lagged, coords, nearest.reshape(ROWS)


def solution(mesh):
    placed = (P("frames", "feats"), P("frames"), P("feats", None), P(), P("frames"))
    return jax.shard_map(
        per_device,
        mesh=mesh,
        in_specs=placed,
        out_specs=(P("frames", "feats"), P("frames", "feats"), P(None, "frames"), P("frames")),
        check_vma=False,
    )
```

```python
import functools

import jax
import jax.numpy as jnp
from jax import lax
from jax.experimental import pallas as pl
from jax.experimental.pallas import tpu as pltpu
from jax.sharding import PartitionSpec as P

MESH = pl.DeviceIdType.MESH
F32 = jnp.float32
BF16 = jnp.bfloat16
I16 = jnp.int16

ROWS = 1536
FB = 512
LAG = 512
TOTAL = 49152
K = 64
C = 256
CH = 256
NCH = ROWS // CH
NALL = (ROWS + LAG) // CH
HF = FB // 2
LEVELS = 32767.0

OFFSETS = ((0, 0), (1, 0), (3, 0), (1, 1))
UNITS = (
    (0, 0, 0), (0, 0, 1), (1, 0, 0), (2, 0, 0), (3, 0, 0), (1, 0, 1), (2, 0, 1), (2, 1, 0),
    (2, 1, 1), (0, 3, 0), (1, 3, 0), (2, 3, 0), (0, 3, 1), (1, 3, 1), (2, 3, 1), (3, 0, 1),
)
LAG_SLOT = {0: 0, 1: 1, 3: 2}
NU = len(UNITS)
XS = 32


def dot(a, b, dims, precision=None):
    return lax.dot_general(a, b, ((dims[:1], dims[1:]), ((), ())), precision=precision, preferred_element_type=F32)


def kernel(
    x_ref, idx_ref, proj_ref, ids_ref, prev_ref,
    both_ref, coords_ref, near_ref,
    xb, lb, u, cx, s1, s1s, r1, r1s, s2, s2s, r2, r2s, zf, zfs, zs, zss, zr, zrs, es, ec, ecs, oc, ocs,
    cpart, crecv, csum, call, cen, cenr, cenall,
    ysend, yrecv, fsend, frecv, hsend, hrecv,
    cxsend, cxrecv, s1send, s1recv, s2send, s2recv, zfsend, zfrecv, zsend, zrecv, esend, erecv,
    psend, precv, gsend, grecv, nsend, nrecv, msend, mrecv,
):
    p = lax.axis_index("frames")
    q = lax.axis_index("feats")
    zh, x, c = p // 8, (p // 2) % 4, p % 2
    y, zl = q // 2, q % 2

    def at(zh_, x_, c_):
        return zh_ * 8 + x_ * 2 + c_

    xp = (at(zh, (x + 1) % 4, c), q)
    xm = (at(zh, (x + 3) % 4, c), q)
    core = (at(zh, x, 1 - c), q)

    def yto(t):
        return (p, ((y + t) % 4) * 2 + zl)

    yp, ym = yto(1), yto(3)
    zo = (p, y * 2 + 1 - zl)
    before = ((p + 31) % 32, q)

    def remote(src, dst, ss, rs, dev):
        return pltpu.make_async_remote_copy(
            src_ref=src, dst_ref=dst, send_sem=ss, recv_sem=rs, device_id=dev, device_id_type=MESH
        )

    barrier = pltpu.get_barrier_semaphore()
    peers = [core, zo, before, ((p + 1) % 32, q)]
    peers += [yto(t) for t in (1, 2, 3)]
    peers += [(at(zh, (x + t) % 4, c), q) for t in (1, 2, 3)]
    peers += [(at((zh + t) % 4, x, c), q) for t in (1, 2, 3)]
    for dev in peers:
        pl.semaphore_signal(barrier, inc=1, device_id=dev, device_id_type=MESH)
    pl.semaphore_wait(barrier, len(peers))

    sent = []

    def send(src, dst, ss, rs, dev):
        r = remote(src, dst, ss, rs, dev)
        r.start()
        sent.append((r, None))
        return r

    def send_if(cond, src, dst, ss, rs, dev):
        r = remote(src, dst, ss, rs, dev)

        @pl.when(cond)
        def _():
            r.start()

        sent.append((r, cond))
        return r

    def part(slot, h, j):
        return xb.at[slot, pl.ds(h * HF, HF), pl.ds(j * CH, CH)]

    def from_y(w, h, j):
        slot = (1, 2)[w]
        return remote(part(0, h, j), part(slot, h, j), ysend.at[w, h, j], yrecv.at[w, h, j], (ym, yp)[w])

    def to_y(w, h, j):
        if j < NCH:
            r = from_y(w, h, j)
            r.start()
            sent.append((r, None))
        else:
            r = from_y(w, h, j)

            @pl.when(c == 1)
            def _():
                r.start()

            sent.append((r, c == 1))

    def on_chip(slot, h, j):
        if j < NALL - NCH:
            k = (0, 1)[slot == 3]
            rs = (yrecv.at[0, h, NCH + j], frecv.at[h, NCH + j])[slot == 3]
            send_if(c == 1, part(slot, h, j), part(slot, h, NCH + j), hsend.at[k, h, j], rs, core)

    def forward(h, j):
        r = remote(part(1, h, j), part(3, h, j), fsend.at[h, j], frecv.at[h, j], zo)
        if j < NCH:
            from_y(0, h, j).wait_recv()
            r.start()
            sent.append((r, None))
            on_chip(1, h, j)
        else:
            @pl.when(c == 1)
            def _():
                from_y(0, h, j).wait_recv()
                r.start()

            sent.append((r, c == 1))

    def following(h):
        for j in range(NCH, NALL):
            @pl.when(c == 0)
            def _():
                from_y(0, h, j).wait_recv()

    def from_z(h, j):
        remote(part(1, h, j), part(3, h, j), fsend.at[h, j], frecv.at[h, j], zo).wait_recv()
        on_chip(3, h, j)

    for j in range(NCH):
        xb[0, :, pl.ds(j * CH, CH)] = x_ref[pl.ds(j * CH, CH), :].T
        if j == 1:
            head = send(xb.at[0, :, pl.ds(0, LAG)], xb.at[0, :, pl.ds(ROWS, LAG)], hsend.at[2, 0, 0], hrecv, before)
        if j < 3:
            to_y(0, 0, j)
            to_y(1, 0, j)

    kq = K // 4
    cpart[...] = dot(proj_ref[...], xb[0, :, 0:ROWS], (1, 0))
    crs = []
    for t in (1, 3, 2):
        rows = pl.ds(pl.multiple_of(((y + t) % 4) * kq, kq), kq)
        crs.append(send(cpart.at[rows, :], crecv.at[t], psend.at[t], precv.at[t], yto(t)))
    for j in range(3, NCH):
        to_y(0, 0, j)
        to_y(1, 0, j)
    own_rows = pl.ds(pl.multiple_of(y * kq, kq), kq)
    first = p * ROWS
    small = {}

    def coords1():
        for r in crs:
            r.wait_recv()
        csum[0] = cpart[own_rows, :] + crecv[1] + crecv[2] + crecv[3]
        small["z"] = send(csum.at[0], csum.at[1], psend.at[4], precv.at[4], zo)

    def coords2():
        small["z"].wait_recv()
        total = csum[0] + csum[1]
        call[own_rows, :] = total
        for t in (1, 3, 2):
            send(call.at[own_rows, :], call.at[own_rows, :], gsend.at[t], grecv.at[t], yto(t))
        pick = (lax.broadcasted_iota(jnp.int32, (ROWS, C), 0) + first == ids_ref[...].reshape(1, C)).astype(F32)
        cen[0] = dot(total, pick, (1, 0), lax.Precision.HIGHEST)
        small["n"] = [send(cen.at[0], cenr.at[0], nsend.at[0], nrecv.at[0], core)]

    def centers1():
        for r in small["n"]:
            r.wait_recv()
        cen[1] = cen[0] + cenr[0]
        small["n"] = [
            send(cen.at[1], cenr.at[t], nsend.at[t], nrecv.at[t], (at(zh, (x + t) % 4, c), q)) for t in (1, 2, 3)
        ]

    def centers2():
        for r in small["n"]:
            r.wait_recv()
        cen[2] = cen[1] + cenr[1] + cenr[2] + cenr[3]
        small["n"] = [
            send(cen.at[2], cenr.at[3 + t], nsend.at[3 + t], nrecv.at[3 + t], (at((zh + t) % 4, x, c), q))
            for t in (1, 2, 3)
        ]

    def centers3():
        for r in small["n"]:
            r.wait_recv()
        cenall[own_rows, :] = cen[2] + cenr[4] + cenr[5] + cenr[6]
        for t in (1, 3, 2):
            send(cenall.at[own_rows, :], cenall.at[own_rows, :], msend.at[t], mrecv.at[t], yto(t))

    def nearest():
        for t in (1, 2, 3):
            frm = pl.ds(pl.multiple_of(((y + 4 - t) % 4) * kq, kq), kq)
            remote(call.at[frm, :], call.at[frm, :], gsend.at[t], grecv.at[t], core).wait_recv()
            remote(cenall.at[frm, :], cenall.at[frm, :], msend.at[t], mrecv.at[t], core).wait_recv()
        coords = call[...]
        coords_ref[...] = coords
        centers = cenall[...]
        ones = jnp.ones((8, K), F32)
        square_y = jnp.sum(coords * coords, axis=0, keepdims=True)
        square_c = dot(centers * centers, ones, (0, 1), lax.Precision.HIGHEST)[:, 0:1]
        cross = dot(centers, coords, (0, 0), lax.Precision.HIGHEST)
        dist = (square_c + square_y - 2.0 * cross) * (1.0 / K)
        near_ref[...] = jnp.minimum(prev_ref[...].reshape(1, ROWS), jnp.min(dist, axis=0, keepdims=True))

    def gather(slot, start, size):
        at_slot = LAG_SLOT[slot]
        feats = pl.ds(start, size)

        def body(i, carry):
            base = pl.multiple_of(i * 256, 256)
            here = idx_ref[pl.ds(base, 256)].reshape(1, 256) - (first + base)
            pick = (lax.broadcasted_iota(jnp.int32, (768, 256), 0) == here).astype(F32).astype(BF16)
            lb[at_slot, feats, pl.ds(base, 256)] = dot(xb[slot, feats, pl.ds(base, 768)], pick, (1, 0)).astype(BF16)
            return carry

        lax.fori_loop(0, ROWS // 256, body, 0)

    def encode(value, out, scale_out):
        top = jnp.maximum(jnp.max(jnp.abs(value), axis=0, keepdims=True), 1e-30)
        scale_out[...] = top * (1.0 / LEVELS)
        out[...] = jnp.round(value * (LEVELS / top)).astype(jnp.int32).astype(I16)

    def decode(code, scale):
        return code[...].astype(jnp.int32).astype(F32) * scale[...]

    cxs, s1w, s2w = {}, {}, {}
    mine = pl.ds(pl.multiple_of(c * 128, 128), 128)
    other = pl.ds(pl.multiple_of((1 - c) * 128, 128), 128)

    def stage0(k):
        a, b, h = UNITS[k]
        left = xb[a, pl.ds(h * HF, HF), 0:ROWS]
        u[k, :, 0:FB] = dot(left, xb[b, :, 0:ROWS], (1, 1))
        u[k, :, FB:2 * FB] = dot(left, lb[LAG_SLOT[b]], (1, 1))
        cxs[k] = send(u.at[k, other, :], cx.at[k], cxsend.at[k], cxrecv.at[k], core)

    def slice_of(xs):
        return pl.ds(pl.multiple_of(c * 128 + xs * XS, XS), XS)

    def stage1(k):
        cxs[k].wait_recv()
        u[k, mine, :] = u[k, mine, :] + cx[k]
        encode(u[k, slice_of((x + 2) % 4), :], s1.at[k], s1s.at[k])
        out = []
        for j, dev in ((0, xp), (1, xm)):
            rows = pl.ds(j * 16, 16)
            out.append(send(s1.at[k, rows, :], r1.at[k, rows, :], s1send.at[k, j, 0], s1recv.at[k, j, 0], dev))
            out.append(send(s1s.at[k], r1s.at[k, j], s1send.at[k, j, 1], s1recv.at[k, j, 1], dev))
        s1w[k] = out

    def stage2(k):
        for r in s1w[k]:
            r.wait_recv()
        out = []
        for j, dev, xs in ((0, xp, (x + 1) % 4), (1, xm, (x + 3) % 4)):
            value = u[k, slice_of(xs), :]
            half = decode(r1.at[k, pl.ds(j * 16, 16), :], r1s.at[k, j])
            near, far = (value[0:16] + half, value[16:32]) if j == 0 else (value[0:16], value[16:32] + half)
            encode(jnp.concatenate([near, far], axis=0), s2.at[k, j], s2s.at[k, j])
            out.append(send(s2.at[k, j], r2.at[k, j], s2send.at[k, j, 0], s2recv.at[k, j, 0], dev))
            out.append(send(s2s.at[k, j], r2s.at[k, j], s2send.at[k, j, 1], s2recv.at[k, j, 1], dev))
        s2w[k] = out

    def z_owner(k):
        return (y + OFFSETS[UNITS[k][0]][0]) % 4

    def z_halves(k):
        out = []
        for j, t in ((0, 1), (1, 3)):
            cols = pl.ds(j * FB, FB)
            dev = (at((zh + t) % 4, x, c), q)
            out.append(remote(zs.at[k, :, cols], zf.at[k], zfsend.at[k, j, 0], zfrecv.at[k, 0], dev))
            out.append(remote(zss.at[k, :, cols], zfs.at[k], zfsend.at[k, j, 1], zfrecv.at[k, 1], dev))
        return out

    def z_last(k, j):
        dev = (at(z_owner(k), x, c), q)
        return (
            remote(zs.at[k], zr.at[k, j], zsend.at[k, 0], zrecv.at[k, j, 0], dev),
            remote(zss.at[k], zrs.at[k, j], zsend.at[k, 1], zrecv.at[k, j, 1], dev),
        )

    def z_place(k):
        return (zh + 4 - z_owner(k)) % 4

    def stage3(k):
        for r in s2w[k]:
            r.wait_recv()
        rows = slice_of(x)
        es[k] = u[k, rows, :] + decode(r2.at[k, 0], r2s.at[k, 0]) + decode(r2.at[k, 1], r2s.at[k, 1])

        @pl.when(z_place(k) == 2)
        def _():
            encode(es[k], zs.at[k], zss.at[k])
            for r in z_halves(k):
                r.start()

    def stage4(k):
        for j, place in ((0, 1), (1, 3)):
            @pl.when(z_place(k) == place)
            def _():
                for r in z_halves(k)[:2]:
                    r.wait_recv()
                cols = pl.ds((1 - j) * FB, FB)
                es[k, :, cols] = es[k, :, cols] + decode(zf.at[k], zfs.at[k])
                encode(es[k], zs.at[k], zss.at[k])
                for r in z_last(k, j):
                    r.start()

    def e_send(k):
        a, b, h = UNITS[k]
        rowblock = z_owner(k) * 2 + (zl + OFFSETS[a][1]) % 2
        colblock = ((y + OFFSETS[b][0]) % 4) * 2 + (zl + OFFSETS[b][1]) % 2
        owner = rowblock * 4 + h * 2 + c
        pairs = ((ec.at[k], oc.at[x]), (ecs.at[k], ocs.at[x]))
        far = [remote(src, dst, esend.at[k, i], erecv.at[i], (owner, colblock)) for i, (src, dst) in enumerate(pairs)]
        return owner, b == 0, pairs, far

    def stage5(k):
        @pl.when(z_place(k) == 0)
        def _():
            total = es[k]
            for j in range(2):
                for r in z_last(k, j):
                    r.wait_recv()
                total = total + decode(zr.at[k, j], zrs.at[k, j])
            encode(total / TOTAL, ec.at[k], ecs.at[k])
            owner, own_column, pairs, far = e_send(k)
            if own_column:
                @pl.when(owner == p)
                def _():
                    for i, (src, dst) in enumerate(pairs):
                        pltpu.make_async_copy(src, dst, erecv.at[i]).start()

                @pl.when(owner != p)
                def _():
                    for r in far:
                        r.start()
            else:
                for r in far:
                    r.start()

    def finish(k):
        @pl.when(z_place(k) == 2)
        def _():
            for r in z_halves(k):
                r.wait_send()

        @pl.when(z_place(k) % 2 == 1)
        def _():
            for r in z_last(k, 0):
                r.wait_send()

        owner, own_column, _, far = e_send(k)
        away = z_place(k) == 0
        if own_column:
            away = away & (owner != p)

        @pl.when(away)
        def _():
            for r in far:
                r.wait_send()

    forward(0, 0)
    head.wait_recv()
    for h in (0, 1):
        for j in range(NCH, NALL):
            to_y(0, h, j)
    forward(0, 1)
    gather(0, 0, FB)
    forward(0, 2)
    stage0(0)
    stage0(1)
    forward(0, 3)
    for j in range(NCH):
        to_y(0, 1, j)
        to_y(1, 1, j)
    stage1(0)
    from_z(0, 0)
    forward(0, 4)
    stage1(1)
    from_z(0, 1)
    forward(0, 5)
    stage2(0)
    stage2(1)
    forward(0, 6)
    forward(0, 7)
    coords1()
    for j in range(NCH):
        from_y(1, 0, j).wait_recv()
    stage0(2)
    forward(1, 6)
    forward(1, 7)
    stage0(3)
    stage3(0)
    stage3(1)
    forward(1, 0)
    stage1(2)
    stage1(3)
    coords2()
    forward(1, 1)
    following(0)
    gather(1, 0, HF)
    stage2(2)
    stage2(3)
    forward(1, 2)
    for j in range(2, NCH):
        from_z(0, j)
    stage0(4)
    stage4(0)
    stage4(1)
    forward(1, 3)
    centers1()
    stage1(4)
    for j in range(NCH, NALL):
        from_z(0, j)
    from_z(1, 0)
    from_z(1, 1)
    gather(3, 0, HF)
    forward(1, 4)
    stage3(2)
    stage3(3)
    stage2(4)
    forward(1, 5)
    stage5(0)
    stage5(1)
    centers2()
    for j in range(NCH):
        from_y(1, 1, j).wait_recv()

    def ready(k):
        if k == 7:
            following(1)
            gather(1, HF, HF)
        if k == 9:
            for j in range(2, NALL):
                from_z(1, j)
            gather(3, HF, HF)

    def run(stage, k):
        if 5 <= k < NU:
            stage(k)

    for step in range(5, NU + 9):
        if step < NU:
            ready(step)
            stage0(step)
        run(stage1, step - 1)
        run(stage2, step - 3)
        run(stage3, step - 5)
        run(stage4, step - 7)
        run(stage5, step - 9)
        if step == 5:
            stage3(4)
        if step == 6:
            stage4(2)
            stage4(3)
        if step == 8:
            stage4(4)
            centers3()
        if step == 9:
            stage5(2)
            stage5(3)
        if step == 11:
            stage5(4)
        if step == NU:
            nearest()

    pltpu.make_async_copy(oc, oc, erecv.at[0]).wait()
    pltpu.make_async_copy(ocs, ocs, erecv.at[1]).wait()
    for j in range(4):
        both_ref[pl.ds(j * XS, XS), :] = decode(oc.at[j], ocs.at[j])
    for r, cond in sent:
        if cond is None:
            r.wait_send()
        else:
            @pl.when(cond)
            def _(r=r):
                r.wait_send()
    for k in range(NU):
        finish(k)


def split(both_ref, coords_in, near_in, inst_ref, lag_ref, coords_ref, near_ref):
    inst_ref[...] = both_ref[:, 0:FB]
    lag_ref[...] = both_ref[:, FB:2 * FB]
    coords_ref[...] = coords_in[...]
    near_ref[...] = near_in[...].reshape(ROWS)


def per_device(frames_data, lag_index, projection, center_ids, nearest_prev):
    vmem = pl.BlockSpec(memory_space=pltpu.VMEM)
    dma = pltpu.SemaphoreType.DMA
    wide = 2 * FB
    both, coords, nearest = pl.pallas_call(
        kernel,
        out_shape=[
            jax.ShapeDtypeStruct((128, wide), F32),
            jax.ShapeDtypeStruct((K, ROWS), F32),
            jax.ShapeDtypeStruct((1, ROWS), F32),
        ],
        in_specs=[vmem] * 5,
        out_specs=[vmem] * 3,
        scratch_shapes=[
            pltpu.VMEM((4, FB, ROWS + LAG), BF16),
            pltpu.VMEM((3, FB, ROWS), BF16),
            pltpu.VMEM((NU, HF, wide), F32),
            pltpu.VMEM((NU, 128, wide), F32),
            pltpu.VMEM((NU, XS, wide), I16),
            pltpu.VMEM((NU, 1, wide), F32),
            pltpu.VMEM((NU, XS, wide), I16),
            pltpu.VMEM((NU, 2, 1, wide), F32),
            pltpu.VMEM((NU, 2, XS, wide), I16),
            pltpu.VMEM((NU, 2, 1, wide), F32),
            pltpu.VMEM((NU, 2, XS, wide), I16),
            pltpu.VMEM((NU, 2, 1, wide), F32),
            pltpu.VMEM((NU, XS, FB), I16),
            pltpu.VMEM((NU, 1, FB), F32),
            pltpu.VMEM((NU, XS, wide), I16),
            pltpu.VMEM((NU, 1, wide), F32),
            pltpu.VMEM((NU, 2, XS, wide), I16),
            pltpu.VMEM((NU, 2, 1, wide), F32),
            pltpu.VMEM((NU, XS, wide), F32),
            pltpu.VMEM((NU, XS, wide), I16),
            pltpu.VMEM((NU, 1, wide), F32),
            pltpu.VMEM((4, XS, wide), I16),
            pltpu.VMEM((4, 1, wide), F32),
            pltpu.VMEM((K, ROWS), F32),
            pltpu.VMEM((4, K // 4, ROWS), F32),
            pltpu.VMEM((2, K // 4, ROWS), F32),
            pltpu.VMEM((K, ROWS), F32),
            pltpu.VMEM((3, K // 4, C), F32),
            pltpu.VMEM((7, K // 4, C), F32),
            pltpu.VMEM((K, C), F32),
            dma((2, 2, NALL)), dma((2, 2, NALL)), dma((2, NALL)), dma((2, NALL)), dma((3, 2, 2)), dma(()),
            dma((NU,)), dma((NU,)), dma((NU, 2, 2)), dma((NU, 2, 2)), dma((NU, 2, 2)), dma((NU, 2, 2)),
            dma((NU, 2, 2)), dma((NU, 2)), dma((NU, 2)), dma((NU, 2, 2)), dma((NU, 2)), dma((2,)),
            dma((5,)), dma((5,)), dma((4,)), dma((4,)), dma((7,)), dma((7,)), dma((4,)), dma((4,)),
        ],
        compiler_params=pltpu.CompilerParams(collective_id=0, has_side_effects=True, vmem_limit_bytes=60 * 2**20),
        name="tica",
    )(
        frames_data,
        lag_index,
        projection.T,
        center_ids,
        nearest_prev,
    )
    return pl.pallas_call(
        split,
        out_shape=[
            jax.ShapeDtypeStruct((128, FB), F32),
            jax.ShapeDtypeStruct((128, FB), F32),
            jax.ShapeDtypeStruct((K, ROWS), F32),
            jax.ShapeDtypeStruct((ROWS,), F32),
        ],
        in_specs=[vmem] * 3,
        out_specs=[vmem] * 4,
        name="split",
    )(both, coords, nearest)


def solution(mesh):
    placed = (P("frames", "feats"), P("frames"), P("feats", None), P(), P("frames"))
    return jax.shard_map(
        per_device,
        mesh=mesh,
        in_specs=placed,
        out_specs=(P("frames", "feats"), P("frames", "feats"), P(None, "frames"), P("frames")),
        check_vma=False,
    )
```

```python
import functools

import jax
import jax.numpy as jnp
from jax import lax
from jax.experimental import pallas as pl
from jax.experimental.pallas import tpu as pltpu
from jax.sharding import PartitionSpec as P

MESH = pl.DeviceIdType.MESH
F32 = jnp.float32
BF16 = jnp.bfloat16
I16 = jnp.int16

ROWS = 1536
FB = 512
LAG = 512
TOTAL = 49152
K = 64
C = 256
CH = 256
NCH = ROWS // CH
NALL = (ROWS + LAG) // CH
HF = FB // 2
LEVELS = 32767.0

OFFSETS = ((0, 0), (1, 0), (3, 0), (1, 1))
UNITS = (
    (0, 0, 0), (0, 0, 1), (1, 0, 0), (2, 0, 0), (3, 0, 0), (1, 0, 1), (2, 0, 1), (2, 1, 0),
    (2, 1, 1), (0, 3, 0), (1, 3, 0), (2, 3, 0), (0, 3, 1), (1, 3, 1), (2, 3, 1), (3, 0, 1),
)
LAG_SLOT = {0: 0, 1: 1, 3: 2}
NU = len(UNITS)
DIRECT = 5
XS = 32


def dot(a, b, dims, precision=None):
    return lax.dot_general(a, b, ((dims[:1], dims[1:]), ((), ())), precision=precision, preferred_element_type=F32)


def kernel(
    x_ref, idx_ref, proj_ref, ids_ref, prev_ref,
    both_ref, coords_ref, near_ref,
    xb, lb, u, cx, s1, s1s, r1, r1s, s2, s2s, r2, r2s, zf, zfs, zs, zss, zr, zrs, es, ec, ecs, oc, ocs,
    cpart, crecv, csum, call, cen, cenr, cenall,
    ysend, yrecv, fsend, frecv, hsend, hrecv,
    cxsend, cxrecv, s1send, s1recv, s2send, s2recv, zfsend, zfrecv, zsend, zrecv, esend, erecv,
    psend, precv, gsend, grecv, nsend, nrecv, msend, mrecv,
):
    p = lax.axis_index("frames")
    q = lax.axis_index("feats")
    zh, x, c = p // 8, (p // 2) % 4, p % 2
    y, zl = q // 2, q % 2

    def at(zh_, x_, c_):
        return zh_ * 8 + x_ * 2 + c_

    xp = (at(zh, (x + 1) % 4, c), q)
    xm = (at(zh, (x + 3) % 4, c), q)
    core = (at(zh, x, 1 - c), q)

    def yto(t):
        return (p, ((y + t) % 4) * 2 + zl)

    yp, ym = yto(1), yto(3)
    zo = (p, y * 2 + 1 - zl)
    before = ((p + 31) % 32, q)

    def remote(src, dst, ss, rs, dev):
        return pltpu.make_async_remote_copy(
            src_ref=src, dst_ref=dst, send_sem=ss, recv_sem=rs, device_id=dev, device_id_type=MESH
        )

    barrier = pltpu.get_barrier_semaphore()
    peers = [core, zo, before, ((p + 1) % 32, q)]
    peers += [yto(t) for t in (1, 2, 3)]
    peers += [(at(zh, (x + t) % 4, c), q) for t in (1, 2, 3)]
    peers += [(at((zh + t) % 4, x, c), q) for t in (1, 2, 3)]
    for dev in peers:
        pl.semaphore_signal(barrier, inc=1, device_id=dev, device_id_type=MESH)
    pl.semaphore_wait(barrier, len(peers))

    sent = []

    def send(src, dst, ss, rs, dev):
        r = remote(src, dst, ss, rs, dev)
        r.start()
        sent.append((r, None))
        return r

    def send_if(cond, src, dst, ss, rs, dev):
        r = remote(src, dst, ss, rs, dev)

        @pl.when(cond)
        def _():
            r.start()

        sent.append((r, cond))
        return r

    def part(slot, h, j):
        return xb.at[slot, pl.ds(h * HF, HF), pl.ds(j * CH, CH)]

    def from_y(w, h, j):
        slot = (1, 2)[w]
        return remote(part(0, h, j), part(slot, h, j), ysend.at[w, h, j], yrecv.at[w, h, j], (ym, yp)[w])

    def to_y(w, h, j):
        if j < NCH:
            r = from_y(w, h, j)
            r.start()
            sent.append((r, None))
        else:
            r = from_y(w, h, j)

            @pl.when(c == 1)
            def _():
                r.start()

            sent.append((r, c == 1))

    def on_chip(slot, h, j):
        if j < NALL - NCH:
            k = (0, 1)[slot == 3]
            rs = (yrecv.at[0, h, NCH + j], frecv.at[h, NCH + j])[slot == 3]
            send_if(c == 1, part(slot, h, j), part(slot, h, NCH + j), hsend.at[k, h, j], rs, core)

    def forward(h, j):
        r = remote(part(1, h, j), part(3, h, j), fsend.at[h, j], frecv.at[h, j], zo)
        if j < NCH:
            from_y(0, h, j).wait_recv()
            r.start()
            sent.append((r, None))
            on_chip(1, h, j)
        else:
            @pl.when(c == 1)
            def _():
                from_y(0, h, j).wait_recv()
                r.start()

            sent.append((r, c == 1))

    def following(h):
        for j in range(NCH, NALL):
            @pl.when(c == 0)
            def _():
                from_y(0, h, j).wait_recv()

    def from_z(h, j):
        remote(part(1, h, j), part(3, h, j), fsend.at[h, j], frecv.at[h, j], zo).wait_recv()
        on_chip(3, h, j)

    for j in range(NCH):
        xb[0, :, pl.ds(j * CH, CH)] = x_ref[pl.ds(j * CH, CH), :].T
        if j == 1:
            head = send(xb.at[0, :, pl.ds(0, LAG)], xb.at[0, :, pl.ds(ROWS, LAG)], hsend.at[2, 0, 0], hrecv, before)
        if j < 3:
            to_y(0, 0, j)
            to_y(1, 0, j)

    kq = K // 4
    for j in range(3, NCH):
        to_y(0, 0, j)
        to_y(1, 0, j)
    own_rows = pl.ds(pl.multiple_of(y * kq, kq), kq)
    first = p * ROWS
    small = {}

    crs = []

    def coords0():
        cpart[...] = dot(proj_ref[...], xb[0, :, 0:ROWS], (1, 0))
        for t in (1, 3, 2):
            rows = pl.ds(pl.multiple_of(((y + t) % 4) * kq, kq), kq)
            crs.append(send(cpart.at[rows, :], crecv.at[t], psend.at[t], precv.at[t], yto(t)))

    def coords1():
        for r in crs:
            r.wait_recv()
        csum[0] = cpart[own_rows, :] + crecv[1] + crecv[2] + crecv[3]
        small["z"] = send(csum.at[0], csum.at[1], psend.at[4], precv.at[4], zo)

    def coords2():
        small["z"].wait_recv()
        total = csum[0] + csum[1]
        call[own_rows, :] = total
        for t in (1, 3, 2):
            send(call.at[own_rows, :], call.at[own_rows, :], gsend.at[t], grecv.at[t], yto(t))
        pick = (lax.broadcasted_iota(jnp.int32, (ROWS, C), 0) + first == ids_ref[...].reshape(1, C)).astype(F32)
        cen[0] = dot(total, pick, (1, 0), lax.Precision.HIGHEST)
        small["n"] = [send(cen.at[0], cenr.at[0], nsend.at[0], nrecv.at[0], core)]

    def centers1():
        for r in small["n"]:
            r.wait_recv()
        cen[1] = cen[0] + cenr[0]
        small["n"] = [
            send(cen.at[1], cenr.at[t], nsend.at[t], nrecv.at[t], (at(zh, (x + t) % 4, c), q)) for t in (1, 2, 3)
        ]

    def centers2():
        for r in small["n"]:
            r.wait_recv()
        cen[2] = cen[1] + cenr[1] + cenr[2] + cenr[3]
        small["n"] = [
            send(cen.at[2], cenr.at[3 + t], nsend.at[3 + t], nrecv.at[3 + t], (at((zh + t) % 4, x, c), q))
            for t in (1, 2, 3)
        ]

    def centers3():
        for r in small["n"]:
            r.wait_recv()
        cenall[own_rows, :] = cen[2] + cenr[4] + cenr[5] + cenr[6]
        for t in (1, 3, 2):
            send(cenall.at[own_rows, :], cenall.at[own_rows, :], msend.at[t], mrecv.at[t], yto(t))

    def nearest():
        for t in (1, 2, 3):
            frm = pl.ds(pl.multiple_of(((y + 4 - t) % 4) * kq, kq), kq)
            remote(call.at[frm, :], call.at[frm, :], gsend.at[t], grecv.at[t], core).wait_recv()
            remote(cenall.at[frm, :], cenall.at[frm, :], msend.at[t], mrecv.at[t], core).wait_recv()
        coords = call[...]
        coords_ref[...] = coords
        centers = cenall[...]
        ones = jnp.ones((8, K), F32)
        square_y = jnp.sum(coords * coords, axis=0, keepdims=True)
        square_c = dot(centers * centers, ones, (0, 1), lax.Precision.HIGHEST)[:, 0:1]
        cross = dot(centers, coords, (0, 0), lax.Precision.HIGHEST)
        dist = (square_c + square_y - 2.0 * cross) * (1.0 / K)
        near_ref[...] = jnp.minimum(prev_ref[...].reshape(1, ROWS), jnp.min(dist, axis=0, keepdims=True))

    def gather(slot, start, size):
        at_slot = LAG_SLOT[slot]
        feats = pl.ds(start, size)

        def body(i, carry):
            base = pl.multiple_of(i * 256, 256)
            here = idx_ref[pl.ds(base, 256)].reshape(1, 256) - (first + base)
            pick = (lax.broadcasted_iota(jnp.int32, (768, 256), 0) == here).astype(F32).astype(BF16)
            lb[at_slot, feats, pl.ds(base, 256)] = dot(xb[slot, feats, pl.ds(base, 768)], pick, (1, 0)).astype(BF16)
            return carry

        lax.fori_loop(0, ROWS // 256, body, 0)

    def encode(value, out, scale_out):
        top = jnp.maximum(jnp.max(jnp.abs(value), axis=0, keepdims=True), 1e-30)
        scale_out[...] = top * (1.0 / LEVELS)
        out[...] = jnp.round(value * (LEVELS / top)).astype(jnp.int32).astype(I16)

    def decode(code, scale):
        return code[...].astype(jnp.int32).astype(F32) * scale[...]

    cxs, s1w, s2w = {}, {}, {}
    mine = pl.ds(pl.multiple_of(c * 128, 128), 128)
    other = pl.ds(pl.multiple_of((1 - c) * 128, 128), 128)

    def stage0(k):
        a, b, h = UNITS[k]
        left = xb[a, pl.ds(h * HF, HF), 0:ROWS]
        u[k, :, 0:FB] = dot(left, xb[b, :, 0:ROWS], (1, 1))
        u[k, :, FB:2 * FB] = dot(left, lb[LAG_SLOT[b]], (1, 1))
        cxs[k] = send(u.at[k, other, :], cx.at[k], cxsend.at[k], cxrecv.at[k], core)

    def slice_of(xs):
        return pl.ds(pl.multiple_of(c * 128 + xs * XS, XS), XS)

    def stage1(k):
        cxs[k].wait_recv()
        u[k, mine, :] = u[k, mine, :] + cx[k]
        encode(u[k, slice_of((x + 2) % 4), :], s1.at[k], s1s.at[k])
        out = []
        if k >= DIRECT:
            for j, dev, xs in ((0, xp, (x + 1) % 4), (1, xm, (x + 3) % 4)):
                encode(u[k, slice_of(xs), :], s2.at[k, j], s2s.at[k, j])
                out.append(send(s2.at[k, j], r2.at[k, j], s2send.at[k, j, 0], s2recv.at[k, j, 0], dev))
                out.append(send(s2s.at[k, j], r2s.at[k, j], s2send.at[k, j, 1], s2recv.at[k, j, 1], dev))
            dev = (at(zh, (x + 2) % 4, c), q)
            out.append(send(s1.at[k], r1.at[k], s1send.at[k, 0, 0], s1recv.at[k, 0, 0], dev))
            out.append(send(s1s.at[k], r1s.at[k, 0], s1send.at[k, 0, 1], s1recv.at[k, 0, 1], dev))
            s2w[k] = out
            return
        for j, dev in ((0, xp), (1, xm)):
            rows = pl.ds(j * 16, 16)
            out.append(send(s1.at[k, rows, :], r1.at[k, rows, :], s1send.at[k, j, 0], s1recv.at[k, j, 0], dev))
            out.append(send(s1s.at[k], r1s.at[k, j], s1send.at[k, j, 1], s1recv.at[k, j, 1], dev))
        s1w[k] = out

    def stage2(k):
        if k >= DIRECT:
            return
        for r in s1w[k]:
            r.wait_recv()
        out = []
        for j, dev, xs in ((0, xp, (x + 1) % 4), (1, xm, (x + 3) % 4)):
            value = u[k, slice_of(xs), :]
            half = decode(r1.at[k, pl.ds(j * 16, 16), :], r1s.at[k, j])
            near, far = (value[0:16] + half, value[16:32]) if j == 0 else (value[0:16], value[16:32] + half)
            encode(jnp.concatenate([near, far], axis=0), s2.at[k, j], s2s.at[k, j])
            out.append(send(s2.at[k, j], r2.at[k, j], s2send.at[k, j, 0], s2recv.at[k, j, 0], dev))
            out.append(send(s2s.at[k, j], r2s.at[k, j], s2send.at[k, j, 1], s2recv.at[k, j, 1], dev))
        s2w[k] = out

    def z_owner(k):
        return (y + OFFSETS[UNITS[k][0]][0]) % 4

    def z_halves(k):
        out = []
        for j, t in ((0, 1), (1, 3)):
            cols = pl.ds(j * FB, FB)
            dev = (at((zh + t) % 4, x, c), q)
            out.append(remote(zs.at[k, :, cols], zf.at[k], zfsend.at[k, j, 0], zfrecv.at[k, 0], dev))
            out.append(remote(zss.at[k, :, cols], zfs.at[k], zfsend.at[k, j, 1], zfrecv.at[k, 1], dev))
        return out

    def z_last(k, j):
        dev = (at(z_owner(k), x, c), q)
        return (
            remote(zs.at[k], zr.at[k, j], zsend.at[k, 0], zrecv.at[k, j, 0], dev),
            remote(zss.at[k], zrs.at[k, j], zsend.at[k, 1], zrecv.at[k, j, 1], dev),
        )

    def z_place(k):
        return (zh + 4 - z_owner(k)) % 4

    def stage3(k):
        for r in s2w[k]:
            r.wait_recv()
        rows = slice_of(x)
        total = u[k, rows, :] + decode(r2.at[k, 0], r2s.at[k, 0]) + decode(r2.at[k, 1], r2s.at[k, 1])
        if k >= DIRECT:
            es[k] = total + decode(r1.at[k], r1s.at[k, 0])

            @pl.when(z_place(k) != 0)
            def _():
                encode(es[k], zs.at[k], zss.at[k])
                for r in z_last(k, z_place(k) - 1):
                    r.start()

            return
        es[k] = total

        @pl.when(z_place(k) == 2)
        def _():
            encode(es[k], zs.at[k], zss.at[k])
            for r in z_halves(k):
                r.start()

    def stage4(k):
        if k >= DIRECT:
            return
        for j, place in ((0, 1), (1, 3)):
            @pl.when(z_place(k) == place)
            def _():
                for r in z_halves(k)[:2]:
                    r.wait_recv()
                cols = pl.ds((1 - j) * FB, FB)
                es[k, :, cols] = es[k, :, cols] + decode(zf.at[k], zfs.at[k])
                encode(es[k], zs.at[k], zss.at[k])
                for r in z_last(k, j):
                    r.start()

    def e_send(k):
        a, b, h = UNITS[k]
        rowblock = z_owner(k) * 2 + (zl + OFFSETS[a][1]) % 2
        colblock = ((y + OFFSETS[b][0]) % 4) * 2 + (zl + OFFSETS[b][1]) % 2
        owner = rowblock * 4 + h * 2 + c
        pairs = ((ec.at[k], oc.at[x]), (ecs.at[k], ocs.at[x]))
        far = [remote(src, dst, esend.at[k, i], erecv.at[i], (owner, colblock)) for i, (src, dst) in enumerate(pairs)]
        return owner, b == 0, pairs, far

    def stage5(k):
        @pl.when(z_place(k) == 0)
        def _():
            total = es[k]
            for j in range(3 if k >= DIRECT else 2):
                for r in z_last(k, j):
                    r.wait_recv()
                total = total + decode(zr.at[k, j], zrs.at[k, j])
            encode(total / TOTAL, ec.at[k], ecs.at[k])
            owner, own_column, pairs, far = e_send(k)
            if own_column:
                @pl.when(owner == p)
                def _():
                    for i, (src, dst) in enumerate(pairs):
                        pltpu.make_async_copy(src, dst, erecv.at[i]).start()

                @pl.when(owner != p)
                def _():
                    for r in far:
                        r.start()
            else:
                for r in far:
                    r.start()

    def finish(k):
        if k < DIRECT:
            @pl.when(z_place(k) == 2)
            def _():
                for r in z_halves(k):
                    r.wait_send()

        @pl.when((z_place(k) != 0) if k >= DIRECT else (z_place(k) % 2 == 1))
        def _():
            for r in z_last(k, 0):
                r.wait_send()

        owner, own_column, _, far = e_send(k)
        away = z_place(k) == 0
        if own_column:
            away = away & (owner != p)

        @pl.when(away)
        def _():
            for r in far:
                r.wait_send()

    forward(0, 0)
    head.wait_recv()
    for h in (0, 1):
        for j in range(NCH, NALL):
            to_y(0, h, j)
    forward(0, 1)
    gather(0, 0, FB)
    forward(0, 2)
    stage0(0)
    stage0(1)
    forward(0, 3)
    for j in range(NCH):
        to_y(0, 1, j)
        to_y(1, 1, j)
    stage1(0)
    from_z(0, 0)
    coords0()
    forward(0, 4)
    stage1(1)
    from_z(0, 1)
    forward(0, 5)
    stage2(0)
    stage2(1)
    forward(0, 6)
    forward(0, 7)
    for j in range(NCH):
        from_y(1, 0, j).wait_recv()
    stage0(2)
    forward(1, 6)
    forward(1, 7)
    stage0(3)
    stage3(0)
    stage3(1)
    forward(1, 0)
    stage1(2)
    stage1(3)
    forward(1, 1)
    following(0)
    gather(1, 0, HF)
    stage2(2)
    stage2(3)
    forward(1, 2)
    for j in range(2, NCH):
        from_z(0, j)
    stage0(4)
    stage4(0)
    stage4(1)
    forward(1, 3)
    stage1(4)
    for j in range(NCH, NALL):
        from_z(0, j)
    from_z(1, 0)
    from_z(1, 1)
    gather(3, 0, HF)
    forward(1, 4)
    stage3(2)
    stage3(3)
    stage2(4)
    forward(1, 5)
    stage5(0)
    stage5(1)
    for j in range(NCH):
        from_y(1, 1, j).wait_recv()

    def ready(k):
        if k == 7:
            following(1)
            gather(1, HF, HF)
        if k == 9:
            for j in range(2, NALL):
                from_z(1, j)
            gather(3, HF, HF)

    def run(stage, k):
        if 5 <= k < NU:
            stage(k)

    for step in range(5, NU + 9):
        if step < NU:
            ready(step)
            stage0(step)
        run(stage1, step - 1)
        run(stage2, step - 3)
        run(stage3, step - 5)
        run(stage4, step - 7)
        run(stage5, step - 9)
        if step == 5:
            stage3(4)
        if step == 6:
            stage4(2)
            stage4(3)
        if step == 8:
            stage4(4)
        if step == 9:
            stage5(2)
            stage5(3)
        if step == 11:
            stage5(4)
        if step == 6:
            coords1()
        if step == 8:
            coords2()
        if step == 10:
            centers1()
        if step == 12:
            centers2()
        if step == 14:
            centers3()

    nearest()
    pltpu.make_async_copy(oc, oc, erecv.at[0]).wait()
    pltpu.make_async_copy(ocs, ocs, erecv.at[1]).wait()
    for j in range(4):
        both_ref[pl.ds(j * XS, XS), :] = decode(oc.at[j], ocs.at[j])
    for r, cond in sent:
        if cond is None:
            r.wait_send()
        else:
            @pl.when(cond)
            def _(r=r):
                r.wait_send()
    for k in range(NU):
        finish(k)


def split(both_ref, coords_in, near_in, inst_ref, lag_ref, coords_ref, near_ref):
    inst_ref[...] = both_ref[:, 0:FB]
    lag_ref[...] = both_ref[:, FB:2 * FB]
    coords_ref[...] = coords_in[...]
    near_ref[...] = near_in[...].reshape(ROWS)


def per_device(frames_data, lag_index, projection, center_ids, nearest_prev):
    vmem = pl.BlockSpec(memory_space=pltpu.VMEM)
    dma = pltpu.SemaphoreType.DMA
    wide = 2 * FB
    both, coords, nearest = pl.pallas_call(
        kernel,
        out_shape=[
            jax.ShapeDtypeStruct((128, wide), F32),
            jax.ShapeDtypeStruct((K, ROWS), F32),
            jax.ShapeDtypeStruct((1, ROWS), F32),
        ],
        in_specs=[vmem] * 5,
        out_specs=[vmem] * 3,
        scratch_shapes=[
            pltpu.VMEM((4, FB, ROWS + LAG), BF16),
            pltpu.VMEM((3, FB, ROWS), BF16),
            pltpu.VMEM((NU, HF, wide), F32),
            pltpu.VMEM((NU, 128, wide), F32),
            pltpu.VMEM((NU, XS, wide), I16),
            pltpu.VMEM((NU, 1, wide), F32),
            pltpu.VMEM((NU, XS, wide), I16),
            pltpu.VMEM((NU, 2, 1, wide), F32),
            pltpu.VMEM((NU, 2, XS, wide), I16),
            pltpu.VMEM((NU, 2, 1, wide), F32),
            pltpu.VMEM((NU, 2, XS, wide), I16),
            pltpu.VMEM((NU, 2, 1, wide), F32),
            pltpu.VMEM((NU, XS, FB), I16),
            pltpu.VMEM((NU, 1, FB), F32),
            pltpu.VMEM((NU, XS, wide), I16),
            pltpu.VMEM((NU, 1, wide), F32),
            pltpu.VMEM((NU, 3, XS, wide), I16),
            pltpu.VMEM((NU, 3, 1, wide), F32),
            pltpu.VMEM((NU, XS, wide), F32),
            pltpu.VMEM((NU, XS, wide), I16),
            pltpu.VMEM((NU, 1, wide), F32),
            pltpu.VMEM((4, XS, wide), I16),
            pltpu.VMEM((4, 1, wide), F32),
            pltpu.VMEM((K, ROWS), F32),
            pltpu.VMEM((4, K // 4, ROWS), F32),
            pltpu.VMEM((2, K // 4, ROWS), F32),
            pltpu.VMEM((K, ROWS), F32),
            pltpu.VMEM((3, K // 4, C), F32),
            pltpu.VMEM((7, K // 4, C), F32),
            pltpu.VMEM((K, C), F32),
            dma((2, 2, NALL)), dma((2, 2, NALL)), dma((2, NALL)), dma((2, NALL)), dma((3, 2, 2)), dma(()),
            dma((NU,)), dma((NU,)), dma((NU, 2, 2)), dma((NU, 2, 2)), dma((NU, 2, 2)), dma((NU, 2, 2)),
            dma((NU, 2, 2)), dma((NU, 2)), dma((NU, 2)), dma((NU, 3, 2)), dma((NU, 2)), dma((2,)),
            dma((5,)), dma((5,)), dma((4,)), dma((4,)), dma((7,)), dma((7,)), dma((4,)), dma((4,)),
        ],
        compiler_params=pltpu.CompilerParams(collective_id=0, has_side_effects=True, vmem_limit_bytes=60 * 2**20),
        name="tica",
    )(
        frames_data,
        lag_index,
        projection.T,
        center_ids,
        nearest_prev,
    )
    return pl.pallas_call(
        split,
        out_shape=[
            jax.ShapeDtypeStruct((128, FB), F32),
            jax.ShapeDtypeStruct((128, FB), F32),
            jax.ShapeDtypeStruct((K, ROWS), F32),
            jax.ShapeDtypeStruct((ROWS,), F32),
        ],
        in_specs=[vmem] * 3,
        out_specs=[vmem] * 4,
        name="split",
    )(both, coords, nearest)


def solution(mesh):
    placed = (P("frames", "feats"), P("frames"), P("feats", None), P(), P("frames"))
    return jax.shard_map(
        per_device,
        mesh=mesh,
        in_specs=placed,
        out_specs=(P("frames", "feats"), P("frames", "feats"), P(None, "frames"), P("frames")),
        check_vma=False,
    )
```

```python
import functools

import jax
import jax.numpy as jnp
from jax import lax
from jax.experimental import pallas as pl
from jax.experimental.pallas import tpu as pltpu
from jax.sharding import PartitionSpec as P

MESH = pl.DeviceIdType.MESH
F32 = jnp.float32
BF16 = jnp.bfloat16
I16 = jnp.int16

ROWS = 1536
FB = 512
LAG = 512
TOTAL = 49152
K = 64
C = 256
CH = 256
NCH = ROWS // CH
NALL = (ROWS + LAG) // CH
HF = FB // 2
LEVELS = 32767.0

OFFSETS = ((0, 0), (1, 0), (3, 0), (1, 1))
UNITS = (
    (0, 0, 0), (0, 0, 1), (1, 0, 0), (2, 0, 0), (3, 0, 0), (1, 0, 1), (2, 0, 1), (2, 1, 0),
    (2, 1, 1), (0, 3, 0), (1, 3, 0), (2, 3, 0), (0, 3, 1), (1, 3, 1), (2, 3, 1), (3, 0, 1),
)
LAG_SLOT = {0: 0, 1: 1, 3: 2}
NU = len(UNITS)
DIRECT = 5
XS = 32


def dot(a, b, dims, precision=None):
    return lax.dot_general(a, b, ((dims[:1], dims[1:]), ((), ())), precision=precision, preferred_element_type=F32)


def kernel(
    x_ref, idx_ref, proj_ref, ids_ref, prev_ref,
    both_ref, coords_ref, near_ref,
    xb, lb, u, cx, s1, s1s, r1, r1s, s2, s2s, r2, r2s, zf, zfs, zs, zss, zr, zrs, es, ec, ecs, oc, ocs,
    cpart, crecv, csum, call, cen, cenr, cenall,
    ysend, yrecv, fsend, frecv, hsend, hrecv,
    cxsend, cxrecv, s1send, s1recv, s2send, s2recv, zfsend, zfrecv, zsend, zrecv, esend, erecv,
    psend, precv, gsend, grecv, nsend, nrecv, msend, mrecv,
):
    p = lax.axis_index("frames")
    q = lax.axis_index("feats")
    zh, x, c = p // 8, (p // 2) % 4, p % 2
    y, zl = q // 2, q % 2

    def at(zh_, x_, c_):
        return zh_ * 8 + x_ * 2 + c_

    xp = (at(zh, (x + 1) % 4, c), q)
    xm = (at(zh, (x + 3) % 4, c), q)
    core = (at(zh, x, 1 - c), q)

    def yto(t):
        return (p, ((y + t) % 4) * 2 + zl)

    yp, ym = yto(1), yto(3)
    zo = (p, y * 2 + 1 - zl)
    before = ((p + 31) % 32, q)

    def remote(src, dst, ss, rs, dev):
        return pltpu.make_async_remote_copy(
            src_ref=src, dst_ref=dst, send_sem=ss, recv_sem=rs, device_id=dev, device_id_type=MESH
        )

    barrier = pltpu.get_barrier_semaphore()
    peers = [core, zo, before, ((p + 1) % 32, q)]
    peers += [yto(t) for t in (1, 2, 3)]
    peers += [(at(zh, (x + t) % 4, c), q) for t in (1, 2, 3)]
    peers += [(at((zh + t) % 4, x, c), q) for t in (1, 2, 3)]
    for dev in peers:
        pl.semaphore_signal(barrier, inc=1, device_id=dev, device_id_type=MESH)
    pl.semaphore_wait(barrier, len(peers))

    sent = []

    def send(src, dst, ss, rs, dev):
        r = remote(src, dst, ss, rs, dev)
        r.start()
        sent.append((r, None))
        return r

    def send_if(cond, src, dst, ss, rs, dev):
        r = remote(src, dst, ss, rs, dev)

        @pl.when(cond)
        def _():
            r.start()

        sent.append((r, cond))
        return r

    def part(slot, h, j):
        return xb.at[slot, pl.ds(h * HF, HF), pl.ds(j * CH, CH)]

    def from_y(w, h, j):
        slot = (1, 2)[w]
        return remote(part(0, h, j), part(slot, h, j), ysend.at[w, h, j], yrecv.at[w, h, j], (ym, yp)[w])

    def to_y(w, h, j):
        if j < NCH:
            r = from_y(w, h, j)
            r.start()
            sent.append((r, None))
        else:
            r = from_y(w, h, j)

            @pl.when(c == 1)
            def _():
                r.start()

            sent.append((r, c == 1))

    def on_chip(slot, h, j):
        if j < NALL - NCH:
            k = (0, 1)[slot == 3]
            rs = (yrecv.at[0, h, NCH + j], frecv.at[h, NCH + j])[slot == 3]
            send_if(c == 1, part(slot, h, j), part(slot, h, NCH + j), hsend.at[k, h, j], rs, core)

    def forward(h, j):
        r = remote(part(1, h, j), part(3, h, j), fsend.at[h, j], frecv.at[h, j], zo)
        if j < NCH:
            from_y(0, h, j).wait_recv()
            r.start()
            sent.append((r, None))
            on_chip(1, h, j)
        else:
            @pl.when(c == 1)
            def _():
                from_y(0, h, j).wait_recv()
                r.start()

            sent.append((r, c == 1))

    def following(h):
        for j in range(NCH, NALL):
            @pl.when(c == 0)
            def _():
                from_y(0, h, j).wait_recv()

    def from_z(h, j):
        remote(part(1, h, j), part(3, h, j), fsend.at[h, j], frecv.at[h, j], zo).wait_recv()
        on_chip(3, h, j)

    for j in range(NCH):
        xb[0, :, pl.ds(j * CH, CH)] = x_ref[pl.ds(j * CH, CH), :].T
        if j == 1:
            head = send(xb.at[0, :, pl.ds(0, LAG)], xb.at[0, :, pl.ds(ROWS, LAG)], hsend.at[2, 0, 0], hrecv, before)
        if j < 3:
            to_y(0, 0, j)
            to_y(1, 0, j)

    kq = K // 4
    for j in range(3, NCH):
        to_y(0, 0, j)
        to_y(1, 0, j)
    own_rows = pl.ds(pl.multiple_of(y * kq, kq), kq)
    first = p * ROWS
    small = {}

    crs = []

    def coords0():
        cpart[...] = dot(proj_ref[...], xb[0, :, 0:ROWS], (1, 0))
        for t in (1, 3, 2):
            rows = pl.ds(pl.multiple_of(((y + t) % 4) * kq, kq), kq)
            crs.append(send(cpart.at[rows, :], crecv.at[t], psend.at[t], precv.at[t], yto(t)))

    def coords1():
        for r in crs:
            r.wait_recv()
        csum[0] = cpart[own_rows, :] + crecv[1] + crecv[2] + crecv[3]
        small["z"] = send(csum.at[0], csum.at[1], psend.at[4], precv.at[4], zo)

    def coords2():
        small["z"].wait_recv()
        total = csum[0] + csum[1]
        call[own_rows, :] = total
        for t in (1, 3, 2):
            send(call.at[own_rows, :], call.at[own_rows, :], gsend.at[t], grecv.at[t], yto(t))
        pick = (lax.broadcasted_iota(jnp.int32, (ROWS, C), 0) + first == ids_ref[...].reshape(1, C)).astype(F32)
        cen[0] = dot(total, pick, (1, 0), lax.Precision.HIGHEST)
        small["n"] = [send(cen.at[0], cenr.at[0], nsend.at[0], nrecv.at[0], core)]

    def centers1():
        for r in small["n"]:
            r.wait_recv()
        cen[1] = cen[0] + cenr[0]
        small["n"] = [
            send(cen.at[1], cenr.at[t], nsend.at[t], nrecv.at[t], (at(zh, (x + t) % 4, c), q)) for t in (1, 2, 3)
        ]

    def centers2():
        for r in small["n"]:
            r.wait_recv()
        cen[2] = cen[1] + cenr[1] + cenr[2] + cenr[3]
        small["n"] = [
            send(cen.at[2], cenr.at[3 + t], nsend.at[3 + t], nrecv.at[3 + t], (at((zh + t) % 4, x, c), q))
            for t in (1, 2, 3)
        ]

    def centers3():
        for r in small["n"]:
            r.wait_recv()
        cenall[own_rows, :] = cen[2] + cenr[4] + cenr[5] + cenr[6]
        for t in (1, 3, 2):
            send(cenall.at[own_rows, :], cenall.at[own_rows, :], msend.at[t], mrecv.at[t], yto(t))

    def nearest():
        for t in (1, 2, 3):
            frm = pl.ds(pl.multiple_of(((y + 4 - t) % 4) * kq, kq), kq)
            remote(call.at[frm, :], call.at[frm, :], gsend.at[t], grecv.at[t], core).wait_recv()
            remote(cenall.at[frm, :], cenall.at[frm, :], msend.at[t], mrecv.at[t], core).wait_recv()
        coords = call[...]
        coords_ref[...] = coords
        centers = cenall[...]
        ones = jnp.ones((8, K), F32)
        square_y = jnp.sum(coords * coords, axis=0, keepdims=True)
        square_c = dot(centers * centers, ones, (0, 1), lax.Precision.HIGHEST)[:, 0:1]
        cross = dot(centers, coords, (0, 0), lax.Precision.HIGHEST)
        dist = (square_c + square_y - 2.0 * cross) * (1.0 / K)
        near_ref[...] = jnp.minimum(prev_ref[...].reshape(1, ROWS), jnp.min(dist, axis=0, keepdims=True))

    def gather(slot, start, size):
        at_slot = LAG_SLOT[slot]
        feats = pl.ds(start, size)

        def body(i, carry):
            base = pl.multiple_of(i * 256, 256)
            here = idx_ref[pl.ds(base, 256)].reshape(1, 256) - (first + base)
            pick = (lax.broadcasted_iota(jnp.int32, (768, 256), 0) == here).astype(F32).astype(BF16)
            lb[at_slot, feats, pl.ds(base, 256)] = dot(xb[slot, feats, pl.ds(base, 768)], pick, (1, 0)).astype(BF16)
            return carry

        lax.fori_loop(0, ROWS // 256, body, 0)

    def encode(value, out, scale_out):
        top = jnp.maximum(jnp.max(jnp.abs(value), axis=0, keepdims=True), 1e-30)
        scale_out[...] = top * (1.0 / LEVELS)
        out[...] = jnp.round(value * (LEVELS / top)).astype(jnp.int32).astype(I16)

    def decode(code, scale):
        return code[...].astype(jnp.int32).astype(F32) * scale[...]

    cxs, s1w, s2w = {}, {}, {}
    mine = pl.ds(pl.multiple_of(c * 128, 128), 128)
    other = pl.ds(pl.multiple_of((1 - c) * 128, 128), 128)

    def stage0(k):
        a, b, h = UNITS[k]
        left = xb[a, pl.ds(h * HF, HF), 0:ROWS]
        u[k, :, 0:FB] = dot(left, xb[b, :, 0:ROWS], (1, 1))
        u[k, :, FB:2 * FB] = dot(left, lb[LAG_SLOT[b]], (1, 1))
        cxs[k] = send(u.at[k, other, :], cx.at[k], cxsend.at[k], cxrecv.at[k], core)

    def slice_of(xs):
        return pl.ds(pl.multiple_of(c * 128 + xs * XS, XS), XS)

    def stage1(k):
        cxs[k].wait_recv()
        u[k, mine, :] = u[k, mine, :] + cx[k]
        encode(u[k, slice_of((x + 2) % 4), :], s1.at[k], s1s.at[k])
        out = []
        if k >= DIRECT:
            dev = (at(zh, (x + 2) % 4, c), q)
            out.append(send(s1.at[k], r1.at[k], s1send.at[k, 0, 0], s1recv.at[k, 0, 0], dev))
            out.append(send(s1s.at[k], r1s.at[k, 0], s1send.at[k, 0, 1], s1recv.at[k, 0, 1], dev))
            for j, dev, xs in ((0, xp, (x + 1) % 4), (1, xm, (x + 3) % 4)):
                encode(u[k, slice_of(xs), :], s2.at[k, j], s2s.at[k, j])
                out.append(send(s2.at[k, j], r2.at[k, j], s2send.at[k, j, 0], s2recv.at[k, j, 0], dev))
                out.append(send(s2s.at[k, j], r2s.at[k, j], s2send.at[k, j, 1], s2recv.at[k, j, 1], dev))
            s2w[k] = out
            return
        for j, dev in ((0, xp), (1, xm)):
            rows = pl.ds(j * 16, 16)
            out.append(send(s1.at[k, rows, :], r1.at[k, rows, :], s1send.at[k, j, 0], s1recv.at[k, j, 0], dev))
            out.append(send(s1s.at[k], r1s.at[k, j], s1send.at[k, j, 1], s1recv.at[k, j, 1], dev))
        s1w[k] = out

    def stage2(k):
        if k >= DIRECT:
            return
        for r in s1w[k]:
            r.wait_recv()
        out = []
        for j, dev, xs in ((0, xp, (x + 1) % 4), (1, xm, (x + 3) % 4)):
            value = u[k, slice_of(xs), :]
            half = decode(r1.at[k, pl.ds(j * 16, 16), :], r1s.at[k, j])
            near, far = (value[0:16] + half, value[16:32]) if j == 0 else (value[0:16], value[16:32] + half)
            encode(jnp.concatenate([near, far], axis=0), s2.at[k, j], s2s.at[k, j])
            out.append(send(s2.at[k, j], r2.at[k, j], s2send.at[k, j, 0], s2recv.at[k, j, 0], dev))
            out.append(send(s2s.at[k, j], r2s.at[k, j], s2send.at[k, j, 1], s2recv.at[k, j, 1], dev))
        s2w[k] = out

    def z_owner(k):
        return (y + OFFSETS[UNITS[k][0]][0]) % 4

    def z_halves(k):
        out = []
        for j, t in ((0, 1), (1, 3)):
            cols = pl.ds(j * FB, FB)
            dev = (at((zh + t) % 4, x, c), q)
            out.append(remote(zs.at[k, :, cols], zf.at[k], zfsend.at[k, j, 0], zfrecv.at[k, 0], dev))
            out.append(remote(zss.at[k, :, cols], zfs.at[k], zfsend.at[k, j, 1], zfrecv.at[k, 1], dev))
        return out

    def z_last(k, j):
        dev = (at(z_owner(k), x, c), q)
        return (
            remote(zs.at[k], zr.at[k, j], zsend.at[k, 0], zrecv.at[k, j, 0], dev),
            remote(zss.at[k], zrs.at[k, j], zsend.at[k, 1], zrecv.at[k, j, 1], dev),
        )

    def z_place(k):
        return (zh + 4 - z_owner(k)) % 4

    def stage3(k):
        for r in s2w[k]:
            r.wait_recv()
        rows = slice_of(x)
        total = u[k, rows, :] + decode(r2.at[k, 0], r2s.at[k, 0]) + decode(r2.at[k, 1], r2s.at[k, 1])
        if k >= DIRECT:
            es[k] = total + decode(r1.at[k], r1s.at[k, 0])

            @pl.when(z_place(k) != 0)
            def _():
                encode(es[k], zs.at[k], zss.at[k])
                for r in z_last(k, z_place(k) - 1):
                    r.start()

            return
        es[k] = total

        @pl.when(z_place(k) == 2)
        def _():
            encode(es[k], zs.at[k], zss.at[k])
            for r in z_halves(k):
                r.start()

    def stage4(k):
        if k >= DIRECT:
            return
        for j, place in ((0, 1), (1, 3)):
            @pl.when(z_place(k) == place)
            def _():
                for r in z_halves(k)[:2]:
                    r.wait_recv()
                cols = pl.ds((1 - j) * FB, FB)
                es[k, :, cols] = es[k, :, cols] + decode(zf.at[k], zfs.at[k])
                encode(es[k], zs.at[k], zss.at[k])
                for r in z_last(k, j):
                    r.start()

    def e_send(k):
        a, b, h = UNITS[k]
        rowblock = z_owner(k) * 2 + (zl + OFFSETS[a][1]) % 2
        colblock = ((y + OFFSETS[b][0]) % 4) * 2 + (zl + OFFSETS[b][1]) % 2
        owner = rowblock * 4 + h * 2 + c
        pairs = ((ec.at[k], oc.at[x]), (ecs.at[k], ocs.at[x]))
        far = [remote(src, dst, esend.at[k, i], erecv.at[i], (owner, colblock)) for i, (src, dst) in enumerate(pairs)]
        return owner, b == 0, pairs, far

    def stage5(k):
        @pl.when(z_place(k) == 0)
        def _():
            total = es[k]
            for j in range(3 if k >= DIRECT else 2):
                for r in z_last(k, j):
                    r.wait_recv()
                total = total + decode(zr.at[k, j], zrs.at[k, j])
            encode(total / TOTAL, ec.at[k], ecs.at[k])
            owner, own_column, pairs, far = e_send(k)
            if own_column:
                @pl.when(owner == p)
                def _():
                    for i, (src, dst) in enumerate(pairs):
                        pltpu.make_async_copy(src, dst, erecv.at[i]).start()

                @pl.when(owner != p)
                def _():
                    for r in far:
                        r.start()
            else:
                for r in far:
                    r.start()

    def finish(k):
        if k < DIRECT:
            @pl.when(z_place(k) == 2)
            def _():
                for r in z_halves(k):
                    r.wait_send()

        @pl.when((z_place(k) != 0) if k >= DIRECT else (z_place(k) % 2 == 1))
        def _():
            for r in z_last(k, 0):
                r.wait_send()

        owner, own_column, _, far = e_send(k)
        away = z_place(k) == 0
        if own_column:
            away = away & (owner != p)

        @pl.when(away)
        def _():
            for r in far:
                r.wait_send()

    forward(0, 0)
    head.wait_recv()
    for h in (0, 1):
        for j in range(NCH, NALL):
            to_y(0, h, j)
    forward(0, 1)
    gather(0, 0, FB)
    forward(0, 2)
    stage0(0)
    stage0(1)
    forward(0, 3)
    for j in range(NCH):
        to_y(0, 1, j)
        to_y(1, 1, j)
    stage1(0)
    from_z(0, 0)
    coords0()
    forward(0, 4)
    stage1(1)
    from_z(0, 1)
    forward(0, 5)
    stage2(0)
    stage2(1)
    forward(0, 6)
    forward(0, 7)
    for j in range(NCH):
        from_y(1, 0, j).wait_recv()
    stage0(2)
    forward(1, 6)
    forward(1, 7)
    stage0(3)
    stage3(0)
    stage3(1)
    forward(1, 0)
    stage1(2)
    stage1(3)
    forward(1, 1)
    following(0)
    gather(1, 0, HF)
    stage2(2)
    stage2(3)
    forward(1, 2)
    for j in range(2, NCH):
        from_z(0, j)
    stage0(4)
    stage4(0)
    stage4(1)
    forward(1, 3)
    stage1(4)
    for j in range(NCH, NALL):
        from_z(0, j)
    from_z(1, 0)
    from_z(1, 1)
    gather(3, 0, HF)
    forward(1, 4)
    stage3(2)
    stage3(3)
    stage2(4)
    forward(1, 5)
    stage5(0)
    stage5(1)
    for j in range(NCH):
        from_y(1, 1, j).wait_recv()

    def ready(k):
        if k == 7:
            following(1)
            gather(1, HF, HF)
        if k == 9:
            for j in range(2, NALL):
                from_z(1, j)
            gather(3, HF, HF)

    def run(stage, k):
        if 5 <= k < NU:
            stage(k)

    for step in range(5, NU + 9):
        if step < NU:
            ready(step)
            stage0(step)
        run(stage1, step - 1)
        run(stage2, step - 3)
        run(stage3, step - 5)
        run(stage4, step - 7)
        run(stage5, step - 9)
        if step == 5:
            stage3(4)
        if step == 6:
            stage4(2)
            stage4(3)
        if step == 8:
            stage4(4)
        if step == 9:
            stage5(2)
            stage5(3)
        if step == 11:
            stage5(4)
        if step == 6:
            coords1()
        if step == 8:
            coords2()
        if step == 10:
            centers1()
        if step == 12:
            centers2()
        if step == 14:
            centers3()

    nearest()
    pltpu.make_async_copy(oc, oc, erecv.at[0]).wait()
    pltpu.make_async_copy(ocs, ocs, erecv.at[1]).wait()
    for j in range(4):
        both_ref[pl.ds(j * XS, XS), :] = decode(oc.at[j], ocs.at[j])
    for r, cond in sent:
        if cond is None:
            r.wait_send()
        else:
            @pl.when(cond)
            def _(r=r):
                r.wait_send()
    for k in range(NU):
        finish(k)


def split(both_ref, coords_in, near_in, inst_ref, lag_ref, coords_ref, near_ref):
    inst_ref[...] = both_ref[:, 0:FB]
    lag_ref[...] = both_ref[:, FB:2 * FB]
    coords_ref[...] = coords_in[...]
    near_ref[...] = near_in[...].reshape(ROWS)


def per_device(frames_data, lag_index, projection, center_ids, nearest_prev):
    vmem = pl.BlockSpec(memory_space=pltpu.VMEM)
    dma = pltpu.SemaphoreType.DMA
    wide = 2 * FB
    both, coords, nearest = pl.pallas_call(
        kernel,
        out_shape=[
            jax.ShapeDtypeStruct((128, wide), F32),
            jax.ShapeDtypeStruct((K, ROWS), F32),
            jax.ShapeDtypeStruct((1, ROWS), F32),
        ],
        in_specs=[vmem] * 5,
        out_specs=[vmem] * 3,
        scratch_shapes=[
            pltpu.VMEM((4, FB, ROWS + LAG), BF16),
            pltpu.VMEM((3, FB, ROWS), BF16),
            pltpu.VMEM((NU, HF, wide), F32),
            pltpu.VMEM((NU, 128, wide), F32),
            pltpu.VMEM((NU, XS, wide), I16),
            pltpu.VMEM((NU, 1, wide), F32),
            pltpu.VMEM((NU, XS, wide), I16),
            pltpu.VMEM((NU, 2, 1, wide), F32),
            pltpu.VMEM((NU, 2, XS, wide), I16),
            pltpu.VMEM((NU, 2, 1, wide), F32),
            pltpu.VMEM((NU, 2, XS, wide), I16),
            pltpu.VMEM((NU, 2, 1, wide), F32),
            pltpu.VMEM((NU, XS, FB), I16),
            pltpu.VMEM((NU, 1, FB), F32),
            pltpu.VMEM((NU, XS, wide), I16),
            pltpu.VMEM((NU, 1, wide), F32),
            pltpu.VMEM((NU, 3, XS, wide), I16),
            pltpu.VMEM((NU, 3, 1, wide), F32),
            pltpu.VMEM((NU, XS, wide), F32),
            pltpu.VMEM((NU, XS, wide), I16),
            pltpu.VMEM((NU, 1, wide), F32),
            pltpu.VMEM((4, XS, wide), I16),
            pltpu.VMEM((4, 1, wide), F32),
            pltpu.VMEM((K, ROWS), F32),
            pltpu.VMEM((4, K // 4, ROWS), F32),
            pltpu.VMEM((2, K // 4, ROWS), F32),
            pltpu.VMEM((K, ROWS), F32),
            pltpu.VMEM((3, K // 4, C), F32),
            pltpu.VMEM((7, K // 4, C), F32),
            pltpu.VMEM((K, C), F32),
            dma((2, 2, NALL)), dma((2, 2, NALL)), dma((2, NALL)), dma((2, NALL)), dma((3, 2, 2)), dma(()),
            dma((NU,)), dma((NU,)), dma((NU, 2, 2)), dma((NU, 2, 2)), dma((NU, 2, 2)), dma((NU, 2, 2)),
            dma((NU, 2, 2)), dma((NU, 2)), dma((NU, 2)), dma((NU, 3, 2)), dma((NU, 2)), dma((2,)),
            dma((5,)), dma((5,)), dma((4,)), dma((4,)), dma((7,)), dma((7,)), dma((4,)), dma((4,)),
        ],
        compiler_params=pltpu.CompilerParams(collective_id=0, has_side_effects=True, vmem_limit_bytes=60 * 2**20),
        name="tica",
    )(
        frames_data,
        lag_index,
        projection.T,
        center_ids,
        nearest_prev,
    )
    return pl.pallas_call(
        split,
        out_shape=[
            jax.ShapeDtypeStruct((128, FB), F32),
            jax.ShapeDtypeStruct((128, FB), F32),
            jax.ShapeDtypeStruct((K, ROWS), F32),
            jax.ShapeDtypeStruct((ROWS,), F32),
        ],
        in_specs=[vmem] * 3,
        out_specs=[vmem] * 4,
        name="split",
    )(both, coords, nearest)


def solution(mesh):
    placed = (P("frames", "feats"), P("frames"), P("feats", None), P(), P("frames"))
    return jax.shard_map(
        per_device,
        mesh=mesh,
        in_specs=placed,
        out_specs=(P("frames", "feats"), P("frames", "feats"), P(None, "frames"), P("frames")),
        check_vma=False,
    )
```
